32 devices in a mesh: groups: 2 (over y), adapter: 4 (over z), tensor: 2 (over x), sub: 2 (over core).
Axes of the slice: x: 2, y: 2, z: 4, core: 2. Of those that a mesh axis runs over, the one named last changes fastest.
Arguments:
- tokens: bfloat16 [16384, 8192], P(('groups', 'adapter'), ('tensor', 'sub')), parts along dimension 0, may hold values from -6 to 6
- frozen_weight: bfloat16 [8192, 1024], P(('tensor', 'sub'), 'adapter'), may hold values from -0.0625 to 0.0625
- down_tables: bfloat16 [64, 8192, 64], P('adapter', ('tensor', 'sub')), may hold values from -0.0625 to 0.0625
- up_tables: bfloat16 [64, 64, 1024], P('adapter', None, ('tensor', 'sub')), may hold values from -0.75 to 0.75
- cotangent: bfloat16 [16384, 1024], P(('groups', 'adapter'), ('tensor', 'sub')), parts along dimension 0, may hold values from -6 to 6
- block_owner: int32 [128, 1], P(('groups', 'adapter')), parts along dimension 0, may hold values from 0 to 3; in each aligned block of 16 rows (0 to 15, 16 to 31, ...) at most 8 rows name the same one
- block_region: int32 [128], P(('groups', 'adapter')), parts along dimension 0, may hold values from 0 to 15
Outputs:
- projected: bfloat16 [16384, 1024], P(('groups', 'adapter', 'tensor', 'sub')), parts along dimension 0
- grad_down: bfloat16 [128, 8192, 64], P(('groups', 'adapter'), ('tensor', 'sub')), parts along dimension 0
- grad_up: bfloat16 [128, 64, 1024], P(('groups', 'adapter'), None, ('tensor', 'sub')), parts along dimension 0
The draws below stay inside these ranges and needn't reach their ends.
There are 2 independent parts, one for each index of `groups`. The reference program is written for one: setup_inputs(seed, part) draws one part's arguments, and reference() takes and returns one part's arrays. A program takes and returns all parts, laid end to end along the dimension named above; an argument that names none is the same for every part. Nothing has to cross between parts.
Inputs may be any that keep to these rules, and one draw needn't show every extreme that they name: `block_owner`: in each aligned block of 16 entries (the row blocks of one index of adapter) no owner is named more than 8 times, a bound that some block reaches.
All inputs are finite; a program needn't handle non-finite values.
Results may differ from the reference program's by a relative error of at most 0.015.
Values may be sent and summed in bfloat16 or wider, within the bound.
A program may use at most 192 MiB of HBM per device.

```python
import math
import jax
import jax.numpy as jnp
import numpy as np
from jax import lax

D = 8192
KEY_OUTPUTS = 1024
R = 64
BLOCK = 128
REG_DEV = 16
TOK_DEV = 2048
CAP = 8
REGIONS = 64
TOKEN_TOTAL = 8192
NBLK = 64
N_ADAPTER = 4
N_TENSOR = 2
N_SUB = 2


def set_ends(result, own_key, low, largest):
    place = [jax.random.randint(jax.random.fold_in(own_key, axis), (), 0, length) for axis, length in enumerate(result.shape)]
    main_axis = result.shape.index(max(result.shape))
    neighbour = place[:main_axis] + [(place[main_axis] + 1) % result.shape[main_axis]] + place[main_axis + 1:]
    return result.at[tuple(place)].set(low).at[tuple(neighbour)].set(largest)


def block_scale(key, shape, cuts, low, largest):
    level, own = 1.0, jax.random.fold_in(key, 6)
    for axis_at, parts in cuts:
        steps = jnp.exp(jax.random.uniform(jax.random.fold_in(own, axis_at), (parts,), jnp.float32, low / len(cuts), largest / len(cuts)))
        level = level * jnp.repeat(steps, shape[axis_at] // parts).reshape([-1 if axis == axis_at else 1 for axis in range(len(shape))])
    return level


def deal_out(stream_key, own, number, rows, number_of, top, limit, skew):
    order = jax.random.permutation(stream_key, number_of)
    heavy_load, ordinary = load_shares(number_of, rows * top, limit, skew, True), load_shares(number_of, rows * top, limit, skew, False)
    places = jnp.arange(number_of)

    def named(lengths, rotation):
        used = int((lengths > 0).sum())
        fixed = max(1, used // 4)
        moved = fixed + (places - fixed + rotation * (used - fixed)) % max(1, number_of - fixed)
        return jnp.zeros((number_of,), jnp.int32).at[order[jnp.where(places < fixed, places, moved)]].set(jnp.asarray(lengths, jnp.int32))

    lengths = jnp.where(number % 4 == 0, named(heavy_load, number // 4), named(ordinary, number - number // 4 - 1))
    mixed = jax.random.permutation(jax.random.fold_in(own, 3), number_of)
    giver, taker = mixed[0:number_of // 2 * 2:2], mixed[1:number_of // 2 * 2:2]
    margin = jnp.minimum(lengths[giver] - 1, limit - lengths[taker]) // 2
    margin = jnp.where((giver == order[0]) | (taker == order[0]) | (lengths[taker] == 0), 0, jnp.maximum(margin, 0))
    moved = jax.random.randint(jax.random.fold_in(own, 4), (number_of // 2,), 0, 1 << 20) % (margin + 1)
    lengths = lengths.at[giver].add(-moved).at[taker].add(moved)
    members = jnp.searchsorted(jnp.cumsum(lengths), jnp.arange(rows * top), side="right").astype(jnp.int32)
    table = members.reshape(top, rows).T
    table = table[jax.random.permutation(jax.random.fold_in(own, 1), rows)]
    rotation = jax.random.randint(jax.random.fold_in(own, 2), (rows, 1), 0, top)
    return jnp.take_along_axis(table, (jnp.arange(top)[None, :] + rotation) % top, axis=1)


def load_shares(number_of, total, reach, lean, full):
    loads = [(1 << 20) // math.isqrt(grade ** lean) + 1 for grade in range(1, number_of + 1)]
    largest = reach if full else min(reach, max(-(-total // number_of), total * loads[0] // sum(loads)))
    least = 1 if total - largest >= number_of - 1 else 0
    given, rest = [largest] + [least] * (number_of - 1), total - largest - least * (number_of - 1)
    while rest > 0:
        free = [i for i in range(1, number_of) if given[i] < largest] or [i for i in range(1, number_of) if given[i] < reach]
        mass, left = sum([loads[i] for i in free]), rest
        for i in free:
            addition = min(reach - given[i], max(1, left * loads[i] // mass), rest)
            given[i] = given[i] + addition
            rest = rest - addition
    return np.array(given)


def centred(key, dims, spread, limit, cuts=(), kind=jnp.bfloat16):
    entries = jax.random.normal(key, dims, jnp.float32) * spread
    if len(cuts) > 0:
        entries = block_scale(key, dims, cuts, -0.22, 0.18) * entries
    return jnp.clip(entries, min=-limit, max=limit).astype(kind)


def setup_inputs(seed: int = 0, part: int = 0) -> dict:
    splits = jax.random.split(jax.random.key(seed), 8)
    own_keys = jax.random.split(jax.random.fold_in(splits[7], part), 8)
    tokens = centred(own_keys[0], (TOKEN_TOTAL, D), 1.0, 6.0, ((0, 4), (1, 4)))
    frozen_weight = centred(splits[1], (D, KEY_OUTPUTS), D ** -0.5, 0.0625, ((0, 4), (1, 4)))
    down_tables = centred(splits[2], (REGIONS, D, R), D ** -0.5, 0.0625, ((0, 4), (1, 4)))
    up_tables = centred(splits[3], (REGIONS, R, KEY_OUTPUTS), R ** -0.5, 0.75, ((0, 4), (2, 4)))
    cotangent = centred(own_keys[4], (TOKEN_TOTAL, KEY_OUTPUTS), 1.0, 6.0, ((0, 4), (1, 4)))
    block_owner_keys = jax.random.split(jax.random.fold_in(own_keys[5], 1), NBLK // (TOK_DEV // BLOCK))
    block_owner_turns = jax.random.permutation(jax.random.fold_in(own_keys[5], 3), NBLK // (TOK_DEV // BLOCK))
    block_owner = jax.vmap(lambda own, number: deal_out(jax.random.fold_in(own_keys[5], 2), own, number, TOK_DEV // BLOCK, N_ADAPTER, 1, CAP, 2))(block_owner_keys, block_owner_turns).reshape((NBLK, 1))
    block_region = set_ends(jax.random.randint(own_keys[6], (NBLK,), 0, REG_DEV), jax.random.fold_in(own_keys[6], 1), 0, REG_DEV - 1).astype(jnp.int32)
    return dict(tokens=tokens, frozen_weight=frozen_weight, down_tables=down_tables, up_tables=up_tables, cotangent=cotangent, block_owner=block_owner, block_region=block_region)


adapter_scale = 0.25


def reference(tokens, frozen_weight, down_tables, up_tables, cotangent, block_owner, block_region):
    region = (block_owner[:, 0] * REG_DEV + block_region).astype(jnp.int32)
    count = TOKEN_TOTAL // BLOCK
    shares = N_TENSOR * N_SUB
    d_share = D // shares
    kv_share = KEY_OUTPUTS // shares
    tok_blocks = tokens.reshape(count, BLOCK, D).astype(jnp.float32)
    cotangent_blocks = cotangent.reshape(count, BLOCK, KEY_OUTPUTS).astype(jnp.float32)
    block_down = down_tables[region].astype(jnp.float32)
    block_up_weight = up_tables[region].astype(jnp.float32)
    inner_down = jnp.einsum("nbd,ndr->nbr", tok_blocks, block_down)
    rank_down_weight = inner_down.astype(jnp.bfloat16)
    rank_up_weight = (adapter_scale * jnp.einsum("ovq,olq->ovl", cotangent_blocks, block_up_weight)).astype(jnp.bfloat16)
    adapter_keys = (adapter_scale * jnp.einsum("xzm,xms->xzs", rank_down_weight.astype(jnp.float32), block_up_weight)).reshape(TOKEN_TOTAL, KEY_OUTPUTS)
    column_portion = (jnp.arange(KEY_OUTPUTS) // kv_share).astype(jnp.int32)

    def add_share(total, column_slice):
        start = (column_slice * d_share).astype(jnp.int32)
        rows = lax.dynamic_slice_in_dim(tokens, start, d_share, 1)
        weights = lax.dynamic_slice_in_dim(frozen_weight, start, d_share, 0)
        partial_output = jnp.dot(rows, weights, preferred_element_type=jnp.float32)
        partial_output = partial_output + jnp.where((column_portion == column_slice)[None, :], adapter_keys, jnp.float32(0.0))
        rounded = lax.optimization_barrier(partial_output.astype(jnp.bfloat16))
        return total + rounded.astype(jnp.float32), None

    summed, _ = lax.scan(add_share, jnp.zeros((TOKEN_TOTAL, KEY_OUTPUTS), jnp.float32), jnp.arange(shares, dtype=jnp.int32))
    projected = summed.astype(jnp.bfloat16)
    terms_down = jnp.einsum("nbd,nbr->ndr", tok_blocks, rank_up_weight.astype(jnp.float32))
    up_gradient_terms = adapter_scale * jnp.einsum("gdy,gde->gye", rank_down_weight.astype(jnp.float32), cotangent_blocks)
    grad_down = jax.ops.segment_sum(terms_down, region, num_segments=REGIONS).astype(jnp.bfloat16)
    grad_up = jax.ops.segment_sum(up_gradient_terms, region, num_segments=REGIONS).astype(jnp.bfloat16)
    return (projected, grad_down, grad_up)
```

```python
import functools

import jax
import jax.numpy as jnp
from jax import lax
from jax.experimental import pallas as pl
from jax.experimental.pallas import tpu as pltpu
from jax.sharding import PartitionSpec as P

BLOCK = 128


adapter_scale = 0.25

NT = (((1,), (1,)), ((), ()))
NN = (((1,), (0,)), ((), ()))
TN = (((0,), (0,)), ((), ()))


def dot(a, b, dims):
    return lax.dot_general(a, b, dims, preferred_element_type=jnp.float32)


def params():
    return pltpu.CompilerParams(vmem_limit_bytes=40 * 1024 * 1024)


def up_down_parts(region, up_all, cotangent):
    _, rank, cols = up_all.shape
    rows = cotangent.shape[0]

    def kernel(region_ref, up_ref, cot_ref, out_ref):
        out_ref[...] = dot(up_ref[0], cot_ref[...], NT).astype(out_ref.dtype)

    return pl.pallas_call(
        kernel,
        grid_spec=pltpu.PrefetchScalarGridSpec(
            num_scalar_prefetch=1,
            grid=(rows // BLOCK,),
            in_specs=[
                pl.BlockSpec((1, rank, cols), lambda i, r: (r[i], 0, 0)),
                pl.BlockSpec((BLOCK, cols), lambda i, r: (i, 0)),
            ],
            out_specs=pl.BlockSpec((rank, BLOCK), lambda i, r: (0, i)),
        ),
        out_shape=jax.ShapeDtypeStruct((rank, rows), jnp.bfloat16),
        compiler_params=params(),
    )(region, up_all, cotangent)


def summed_terms(order, slot, low, values, scale):
    rank = low.shape[0]
    rows, cols = values.shape
    blocks = rows // BLOCK

    def kernel(order_ref, slot_ref, low_ref, val_ref, out_ref, total):
        i = pl.program_id(0)
        part = dot(low_ref[...], val_ref[...], NN)
        fresh = slot_ref[i] == i

        @pl.when(fresh)
        def _():
            total[...] = part

        @pl.when(jnp.logical_not(fresh))
        def _():
            total[...] += part

        out_ref[0] = (total[...] * scale).astype(out_ref.dtype)

    return pl.pallas_call(
        kernel,
        grid_spec=pltpu.PrefetchScalarGridSpec(
            num_scalar_prefetch=2,
            grid=(blocks,),
            in_specs=[
                pl.BlockSpec((rank, BLOCK), lambda i, o, s: (0, o[i])),
                pl.BlockSpec((BLOCK, cols), lambda i, o, s: (o[i], 0)),
            ],
            out_specs=pl.BlockSpec((1, rank, cols), lambda i, o, s: (s[i], 0, 0)),
            scratch_shapes=[pltpu.VMEM((rank, cols), jnp.float32)],
        ),
        out_shape=jax.ShapeDtypeStruct((blocks, rank, cols), jnp.bfloat16),
        compiler_params=params(),
    )(order, slot, low, values)


def pack(table_at, term_at, kind, tables, terms):
    count = kind.shape[0]
    _, rank, cols = tables.shape

    def kernel(table_ref_at, term_ref_at, kind_ref, table_ref, term_ref, out_ref):
        what = kind_ref[pl.program_id(0)]

        @pl.when(what == 0)
        def _():
            out_ref[...] = table_ref[...]

        @pl.when(what == 1)
        def _():
            out_ref[...] = term_ref[...]

    return pl.pallas_call(
        kernel,
        grid_spec=pltpu.PrefetchScalarGridSpec(
            num_scalar_prefetch=3,
            grid=(count,),
            in_specs=[
                pl.BlockSpec((1, rank, cols), lambda i, a, b, k: (a[i], 0, 0)),
                pl.BlockSpec((1, rank, cols), lambda i, a, b, k: (b[i], 0, 0)),
            ],
            out_specs=pl.BlockSpec((1, rank, cols), lambda i, a, b, k: (i, 0, 0)),
        ),
        out_shape=jax.ShapeDtypeStruct((count, rank, cols), tables.dtype),
        compiler_params=params(),
    )(table_at, term_at, kind, tables, terms)


def inner_parts(got_at, own_at, own, got, tables, tokens):
    _, rank, cols = tables.shape
    rows = tokens.shape[0]

    def kernel(got_ref_at, own_ref_at, own_ref, got_ref, table_ref, tok_ref, out_ref):
        mine = own_ref[pl.program_id(0)] == 1

        @pl.when(mine)
        def _():
            out_ref[...] = dot(table_ref[0], tok_ref[...], NT).astype(out_ref.dtype)

        @pl.when(jnp.logical_not(mine))
        def _():
            out_ref[...] = dot(got_ref[0], tok_ref[...], NT).astype(out_ref.dtype)

    return pl.pallas_call(
        kernel,
        grid_spec=pltpu.PrefetchScalarGridSpec(
            num_scalar_prefetch=3,
            grid=(rows // BLOCK,),
            in_specs=[
                pl.BlockSpec((1, rank, cols), lambda i, g, t, o: (g[i], 0, 0)),
                pl.BlockSpec((1, rank, cols), lambda i, g, t, o: (t[i], 0, 0)),
                pl.BlockSpec((BLOCK, cols), lambda i, g, t, o: (i, 0)),
            ],
            out_specs=pl.BlockSpec((rank, BLOCK), lambda i, g, t, o: (0, i)),
        ),
        out_shape=jax.ShapeDtypeStruct((rank, rows), jnp.bfloat16),
        compiler_params=params(),
    )(got_at, own_at, own, got, tables, tokens)


def owner_sum(got_at, own_at, valid, got, terms, regions):
    consumers = valid.shape[1] - 1
    _, rank, cols = got.shape

    def kernel(got_ref_at, own_ref_at, valid_ref, *refs):
        i = pl.program_id(0)
        out_ref, total = refs[-2], refs[-1]
        total[...] = jnp.zeros_like(total)
        for c in range(consumers + 1):

            @pl.when(valid_ref[i, c] == 1)
            def _(c=c):
                total[...] += refs[c][0].astype(jnp.float32)

        out_ref[0] = total[...].astype(out_ref.dtype)

    def got_map(c, i, g, t, v):
        return (g[i, c], 0, 0)

    return pl.pallas_call(
        kernel,
        grid_spec=pltpu.PrefetchScalarGridSpec(
            num_scalar_prefetch=3,
            grid=(regions,),
            in_specs=[
                pl.BlockSpec((1, rank, cols), functools.partial(got_map, c))
                for c in range(consumers)
            ]
            + [pl.BlockSpec((1, rank, cols), lambda i, g, t, v: (t[i], 0, 0))],
            out_specs=pl.BlockSpec((1, rank, cols), lambda i, g, t, v: (i, 0, 0)),
            scratch_shapes=[pltpu.VMEM((rank, cols), jnp.float32)],
        ),
        out_shape=jax.ShapeDtypeStruct((regions, rank, cols), jnp.bfloat16),
        compiler_params=params(),
    )(got_at, own_at, valid, *([got] * consumers), terms)


def lora_columns(region, low_down, up_all):
    rank, rows = low_down.shape
    cols = up_all.shape[2]

    def kernel(region_ref, low_ref, up_ref, out_ref):
        out_ref[...] = adapter_scale * dot(low_ref[...], up_ref[0], TN)

    return pl.pallas_call(
        kernel,
        grid_spec=pltpu.PrefetchScalarGridSpec(
            num_scalar_prefetch=1,
            grid=(rows // BLOCK,),
            in_specs=[
                pl.BlockSpec((rank, BLOCK), lambda i, r: (0, i)),
                pl.BlockSpec((1, rank, cols), lambda i, r: (r[i], 0, 0)),
            ],
            out_specs=pl.BlockSpec((BLOCK, cols), lambda i, r: (i, 0)),
        ),
        out_shape=jax.ShapeDtypeStruct((rows, cols), jnp.float32),
        compiler_params=params(),
    )(region, low_down, up_all)


def i32(x):
    return x.astype(jnp.int32)


def shards(tokens, frozen_weight, down_tables, up_tables, cotangent, block_owner, block_region):
    lane_index = lax.axis_index(("tensor", "sub"))
    owners = lax.axis_size("adapter")
    me = lax.axis_index("adapter")
    group = lax.axis_index("groups")
    tok_rows, d_part = tokens.shape
    reg_dev, _, rank_width = down_tables.shape
    key_portion = up_tables.shape[2]
    blocks = tok_rows // BLOCK
    slot_limit = max(2, blocks // owners * 2)
    tables = jnp.swapaxes(down_tables, 1, 2)

    region = block_owner[:, 0] * reg_dev + block_region
    named = lax.all_gather(region, ("groups", "adapter"), axis=0, tiled=True)
    named = named.reshape(-1, owners, blocks)
    regions = owners * reg_dev
    present = i32(jnp.any(named[..., None] == jnp.arange(regions), axis=2))
    present = present.reshape(-1, owners, owners, reg_dev)
    counts = jnp.sum(present, axis=-1)
    apart = 1 - jnp.eye(owners, dtype=jnp.int32)
    need = jnp.max((counts + jnp.swapaxes(counts, 1, 2)) * apart)
    here = lax.dynamic_index_in_dim(present, group, 0, False)
    count = lax.dynamic_index_in_dim(counts, group, 0, False)
    before = jnp.arange(reg_dev)[:, None] < jnp.arange(reg_dev)[None, :]
    ranks = jnp.sum(here[..., :, None] * before, axis=-2)
    mine_in = lax.dynamic_index_in_dim(here, me, 0, False)
    mine_of = lax.dynamic_index_in_dim(here, me, 1, False)
    rank_in = lax.dynamic_index_in_dim(ranks, me, 0, False)
    rank_of = lax.dynamic_index_in_dim(ranks, me, 1, False)
    count_in = lax.dynamic_index_in_dim(count, me, 0, False)
    count_of = lax.dynamic_index_in_dim(count, me, 1, False)

    j = jnp.arange(blocks)
    less = region[:, None] < region[None, :]
    tie = (region[:, None] == region[None, :]) & (j[:, None] < j[None, :])
    place = jnp.sum(i32(less | tie), axis=0)
    order = jnp.sum(i32(place[:, None] == j[None, :]) * j[:, None], axis=0)
    first = jnp.sum(i32(less), axis=0)
    slot = jnp.sum(i32(place[:, None] == j[None, :]) * first[:, None], axis=0)
    term_slot = jnp.sum(i32(region[:, None] < jnp.arange(regions)[None, :]), axis=0)
    term_slot = jnp.minimum(term_slot, blocks - 1).reshape(owners, reg_dev)

    up_all = lax.all_gather(up_tables, "adapter", axis=0, tiled=True)
    up_part = up_down_parts(region, up_all, cotangent)
    low_up = lax.psum(up_part, ("tensor", "sub")).astype(jnp.float32)
    low_up = (adapter_scale * low_up).astype(jnp.bfloat16)
    terms = summed_terms(order, slot, low_up, tokens, 1.0)
    weight = lax.all_gather(frozen_weight, "adapter", axis=1, tiled=True)
    frozen_product = jnp.dot(tokens, weight, preferred_element_type=jnp.float32)

    def exchange(slots, tables, terms, tokens):
        s = jnp.arange(slots)
        takes_table = mine_of[:, :, None] * i32(rank_of[:, :, None] == s)
        shifted = rank_in + count_of[:, None]
        takes_term = mine_in[:, :, None] * i32(shifted[:, :, None] == s)
        table_at = jnp.sum(takes_table * jnp.arange(reg_dev)[:, None], axis=1)
        term_at = jnp.sum(takes_term * term_slot[:, :, None], axis=1)
        other = i32(jnp.arange(owners) != me)[:, None]
        kind = jnp.where(
            other * jnp.sum(takes_table, axis=1) > 0,
            0,
            jnp.where(other * jnp.sum(takes_term, axis=1) > 0, 1, 2),
        )
        send = pack(table_at.reshape(-1), term_at.reshape(-1), i32(kind).reshape(-1), tables, terms)
        got = lax.all_to_all(
            send.reshape(owners, slots, rank_width, d_part),
            "adapter", split_axis=0, concat_axis=0, tiled=True,
        ).reshape(owners * slots, rank_width, d_part)
        flat = (jnp.arange(owners)[:, None] * slots + rank_in).reshape(-1)
        own = i32(block_owner[:, 0] == me)
        pick = i32(region[:, None] == jnp.arange(regions))
        got_at = jnp.sum(pick * flat, axis=1) * (1 - own)
        inner = inner_parts(got_at, block_region * own, own, got, tables, tokens)
        remote = mine_of.T * (1 - i32(jnp.arange(owners) == me))
        back_at = (jnp.arange(owners) * slots + count_in)[None, :] + rank_of.T
        own_terms = lax.dynamic_index_in_dim(mine_in, me, 0, False)
        own_slots = lax.dynamic_index_in_dim(term_slot, me, 0, False)
        valid = jnp.concatenate([remote, own_terms[:, None]], axis=1)
        grad = owner_sum(back_at * remote, own_slots * own_terms, valid, got, terms, reg_dev)
        return inner, grad

    full = 2 * slot_limit
    sizes = sorted({-(-full * f // 16) for f in (8, 9, 10, 11, 12, 14, 16)})
    branch = jnp.sum(i32(need > jnp.array(sizes[:-1], jnp.int32)))
    inner, grad_down = lax.switch(
        branch, [functools.partial(exchange, n) for n in sizes], tables, terms, tokens
    )

    low_down = lax.psum(inner, ("tensor", "sub"))
    lora = lora_columns(region, low_down, up_all)
    column_offset = lane_index * key_portion
    owned = lax.dynamic_slice_in_dim(frozen_product, column_offset, key_portion, 1) + lora
    frozen_product = lax.dynamic_update_slice_in_dim(frozen_product, owned, column_offset, 1)
    projected = lax.psum_scatter(
        frozen_product.astype(jnp.bfloat16), ("tensor", "sub"), scatter_dimension=0, tiled=True
    )

    up_terms = summed_terms(order, slot, low_down, cotangent, adapter_scale)
    s = jnp.arange(slot_limit)
    takes = mine_in[:, :, None] * i32(rank_in[:, :, None] == s)
    up_at = jnp.sum(takes * term_slot[:, :, None], axis=1).reshape(-1)
    up_send = jnp.take(up_terms, up_at, axis=0, mode="clip")
    up_got = lax.all_to_all(
        up_send.reshape(owners, slot_limit, rank_width, key_portion),
        "adapter", split_axis=0, concat_axis=0, tiled=True,
    ).reshape(owners * slot_limit, rank_width, key_portion)
    back_at = (jnp.arange(owners) * slot_limit)[None, :] + jnp.minimum(rank_of.T, slot_limit - 1)
    valid = jnp.concatenate([mine_of.T, jnp.zeros((reg_dev, 1), jnp.int32)], axis=1)
    grad_up = owner_sum(
        back_at * mine_of.T, jnp.zeros((reg_dev,), jnp.int32), valid, up_got, up_got, reg_dev
    )
    return (projected, jnp.swapaxes(grad_down, 1, 2), grad_up)


def solution(mesh):
    return jax.shard_map(
        shards,
        mesh=mesh,
        in_specs=(
            P(("groups", "adapter"), ("tensor", "sub")),
            P(("tensor", "sub"), "adapter"),
            P("adapter", ("tensor", "sub"), None),
            P("adapter", None, ("tensor", "sub")),
            P(("groups", "adapter"), ("tensor", "sub")),
            P(("groups", "adapter"), None),
            P(("groups", "adapter")),
        ),
        out_specs=(
            P(("groups", "adapter", "tensor", "sub"), None),
            P(("groups", "adapter"), ("tensor", "sub"), None),
            P(("groups", "adapter"), None, ("tensor", "sub")),
        ),
        check_vma=False,
    )
```

```python
import functools

import jax
import jax.numpy as jnp
from jax import lax
from jax.experimental import pallas as pl
from jax.experimental.pallas import tpu as pltpu
from jax.sharding import PartitionSpec as P

BLOCK = 128


adapter_scale = 0.25

NT = (((1,), (1,)), ((), ()))
NN = (((1,), (0,)), ((), ()))
TN = (((0,), (0,)), ((), ()))


def dot(a, b, dims):
    return lax.dot_general(a, b, dims, preferred_element_type=jnp.float32)


def params():
    return pltpu.CompilerParams(vmem_limit_bytes=40 * 1024 * 1024)


def up_down_parts(region, up_all, cotangent):
    _, rank, cols = up_all.shape
    rows = cotangent.shape[0]

    def kernel(region_ref, up_ref, cot_ref, out_ref):
        out_ref[...] = dot(up_ref[0], cot_ref[...], NT).astype(out_ref.dtype)

    return pl.pallas_call(
        kernel,
        grid_spec=pltpu.PrefetchScalarGridSpec(
            num_scalar_prefetch=1,
            grid=(rows // BLOCK,),
            in_specs=[
                pl.BlockSpec((1, rank, cols), lambda i, r: (r[i], 0, 0)),
                pl.BlockSpec((BLOCK, cols), lambda i, r: (i, 0)),
            ],
            out_specs=pl.BlockSpec((rank, BLOCK), lambda i, r: (0, i)),
        ),
        out_shape=jax.ShapeDtypeStruct((rank, rows), jnp.bfloat16),
        compiler_params=params(),
    )(region, up_all, cotangent)


def summed_terms(order, slot, low, values, scale):
    rank = low.shape[0]
    rows, cols = values.shape
    blocks = rows // BLOCK

    def kernel(order_ref, slot_ref, low_ref, val_ref, out_ref, total):
        i = pl.program_id(0)
        part = dot(low_ref[...], val_ref[...], NN)
        fresh = slot_ref[i] == i

        @pl.when(fresh)
        def _():
            total[...] = part

        @pl.when(jnp.logical_not(fresh))
        def _():
            total[...] += part

        out_ref[0] = (total[...] * scale).astype(out_ref.dtype)

    return pl.pallas_call(
        kernel,
        grid_spec=pltpu.PrefetchScalarGridSpec(
            num_scalar_prefetch=2,
            grid=(blocks,),
            in_specs=[
                pl.BlockSpec((rank, BLOCK), lambda i, o, s: (0, o[i])),
                pl.BlockSpec((BLOCK, cols), lambda i, o, s: (o[i], 0)),
            ],
            out_specs=pl.BlockSpec((1, rank, cols), lambda i, o, s: (s[i], 0, 0)),
            scratch_shapes=[pltpu.VMEM((rank, cols), jnp.float32)],
        ),
        out_shape=jax.ShapeDtypeStruct((blocks, rank, cols), jnp.bfloat16),
        compiler_params=params(),
    )(order, slot, low, values)


def pack(table_at, term_at, kind, tables, terms):
    count = kind.shape[0]
    _, rank, cols = tables.shape

    def kernel(table_ref_at, term_ref_at, kind_ref, table_ref, term_ref, out_ref):
        what = kind_ref[pl.program_id(0)]

        @pl.when(what == 0)
        def _():
            out_ref[...] = table_ref[...]

        @pl.when(what == 1)
        def _():
            out_ref[...] = term_ref[...]

    return pl.pallas_call(
        kernel,
        grid_spec=pltpu.PrefetchScalarGridSpec(
            num_scalar_prefetch=3,
            grid=(count,),
            in_specs=[
                pl.BlockSpec((1, rank, cols), lambda i, a, b, k: (a[i], 0, 0)),
                pl.BlockSpec((1, rank, cols), lambda i, a, b, k: (b[i], 0, 0)),
            ],
            out_specs=pl.BlockSpec((1, rank, cols), lambda i, a, b, k: (i, 0, 0)),
        ),
        out_shape=jax.ShapeDtypeStruct((count, rank, cols), tables.dtype),
        compiler_params=params(),
    )(table_at, term_at, kind, tables, terms)


def inner_parts(got_at, own_at, own, got, tables, tokens):
    _, rank, cols = tables.shape
    rows = tokens.shape[0]

    def kernel(got_ref_at, own_ref_at, own_ref, got_ref, table_ref, tok_ref, out_ref):
        mine = own_ref[pl.program_id(0)] == 1

        @pl.when(mine)
        def _():
            out_ref[...] = dot(table_ref[0], tok_ref[...], NT).astype(out_ref.dtype)

        @pl.when(jnp.logical_not(mine))
        def _():
            out_ref[...] = dot(got_ref[0], tok_ref[...], NT).astype(out_ref.dtype)

    return pl.pallas_call(
        kernel,
        grid_spec=pltpu.PrefetchScalarGridSpec(
            num_scalar_prefetch=3,
            grid=(rows // BLOCK,),
            in_specs=[
                pl.BlockSpec((1, rank, cols), lambda i, g, t, o: (g[i], 0, 0)),
                pl.BlockSpec((1, rank, cols), lambda i, g, t, o: (t[i], 0, 0)),
                pl.BlockSpec((BLOCK, cols), lambda i, g, t, o: (i, 0)),
            ],
            out_specs=pl.BlockSpec((rank, BLOCK), lambda i, g, t, o: (0, i)),
        ),
        out_shape=jax.ShapeDtypeStruct((rank, rows), jnp.bfloat16),
        compiler_params=params(),
    )(got_at, own_at, own, got, tables, tokens)


def owner_sum(got_at, own_at, valid, got, terms, regions):
    consumers = valid.shape[1] - 1
    _, rank, cols = got.shape

    def kernel(got_ref_at, own_ref_at, valid_ref, *refs):
        i = pl.program_id(0)
        out_ref, total = refs[-2], refs[-1]
        total[...] = jnp.zeros_like(total)
        for c in range(consumers + 1):

            @pl.when(valid_ref[i, c] == 1)
            def _(c=c):
                total[...] += refs[c][0].astype(jnp.float32)

        out_ref[0] = total[...].astype(out_ref.dtype)

    def got_map(c, i, g, t, v):
        return (g[i, c], 0, 0)

    return pl.pallas_call(
        kernel,
        grid_spec=pltpu.PrefetchScalarGridSpec(
            num_scalar_prefetch=3,
            grid=(regions,),
            in_specs=[
                pl.BlockSpec((1, rank, cols), functools.partial(got_map, c))
                for c in range(consumers)
            ]
            + [pl.BlockSpec((1, rank, cols), lambda i, g, t, v: (t[i], 0, 0))],
            out_specs=pl.BlockSpec((1, rank, cols), lambda i, g, t, v: (i, 0, 0)),
            scratch_shapes=[pltpu.VMEM((rank, cols), jnp.float32)],
        ),
        out_shape=jax.ShapeDtypeStruct((regions, rank, cols), jnp.bfloat16),
        compiler_params=params(),
    )(got_at, own_at, valid, *([got] * consumers), terms)


def line_exchange(count, step_id, send, mask):
    total, rows, cols = send.shape
    lag, deep = 2, 3

    def kernel(send_ref, mask_ref, got_ref, own_buf, pass_buf, out_buf, load_sem, pass_sem, send_sem, recv_sem):
        me = lax.axis_index("adapter")
        last = lax.axis_size("adapter") - 1
        barrier = pltpu.get_barrier_semaphore()

        @pl.when(me > 0)
        def _():
            pl.semaphore_signal(barrier, inc=1, device_id={"adapter": me - 1}, device_id_type=pl.DeviceIdType.MESH)

        @pl.when(me < last)
        def _():
            pl.semaphore_signal(barrier, inc=1, device_id={"adapter": me + 1}, device_id_type=pl.DeviceIdType.MESH)

        inside = (me > 0) & (me < last)

        @pl.when(inside)
        def _():
            pl.semaphore_wait(barrier, 2)

        @pl.when(jnp.logical_not(inside))
        def _():
            pl.semaphore_wait(barrier, 1)

        def remote(way, t):
            peer = me + 1 if way == 0 else me - 1
            slot = lax.rem(t, deep)
            return pltpu.make_async_remote_copy(
                src_ref=out_buf.at[way, slot],
                dst_ref=got_ref.at[way * count + t],
                send_sem=send_sem.at[way, slot],
                recv_sem=recv_sem.at[way, t],
                device_id={"adapter": peer},
                device_id_type=pl.DeviceIdType.MESH,
            )

        def own_load(way, t):
            return pltpu.make_async_copy(send_ref.at[way * count + t], own_buf.at[way], load_sem.at[way])

        def pass_load(way, t):
            return pltpu.make_async_copy(got_ref.at[way * count + t], pass_buf.at[way], pass_sem.at[way])

        places = (me, last - me)

        def step(i, carry):
            at = [i - lag * place for place in places]
            live = [(t >= 0) & (t < count) for t in at]
            sends = [ok & (place < last) for ok, place in zip(live, places)]
            for way in (0, 1):

                @pl.when(sends[way])
                def _(way=way):
                    own_load(way, at[way]).start()

            for way in (0, 1):

                @pl.when(live[way] & (places[way] > 0))
                def _(way=way):
                    remote(way, at[way]).wait_recv()

                @pl.when(sends[way] & (places[way] > 0))
                def _(way=way):
                    pass_load(way, at[way]).start()

            for way in (0, 1):

                @pl.when(sends[way])
                def _(way=way):
                    t = at[way]
                    slot = lax.rem(t, deep)

                    @pl.when(t >= deep)
                    def _():
                        remote(way, t).wait_send()

                    own_load(way, t).wait()

                    @pl.when(places[way] == 0)
                    def _():
                        out_buf[way, slot] = own_buf[way]

                    @pl.when(places[way] > 0)
                    def _():
                        pass_load(way, t).wait()
                        mine = jnp.broadcast_to(mask_ref[way * count + t], (rows, cols)) > 0
                        out_buf[way, slot] = jnp.where(
                            mine, own_buf[way].astype(jnp.float32), pass_buf[way].astype(jnp.float32)
                        ).astype(out_buf.dtype)

                    remote(way, t).start()

            return carry

        lax.fori_loop(0, count + lag * last, step, 0)
        for way in (0, 1):
            for t in range(count - deep, count):

                @pl.when(places[way] < last)
                def _(way=way, t=t):
                    remote(way, t).wait_send()

    return pl.pallas_call(
        kernel,
        in_specs=[
            pl.BlockSpec(memory_space=pl.ANY),
            pl.BlockSpec(memory_space=pltpu.SMEM),
        ],
        out_specs=pl.BlockSpec(memory_space=pl.ANY),
        out_shape=jax.ShapeDtypeStruct((total, rows, cols), send.dtype),
        scratch_shapes=[
            pltpu.VMEM((2, rows, cols), send.dtype),
            pltpu.VMEM((2, rows, cols), send.dtype),
            pltpu.VMEM((2, deep, rows, cols), send.dtype),
            pltpu.SemaphoreType.DMA((2,)),
            pltpu.SemaphoreType.DMA((2,)),
            pltpu.SemaphoreType.DMA((2, deep)),
            pltpu.SemaphoreType.DMA((2, count)),
        ],
        compiler_params=pltpu.CompilerParams(
            collective_id=step_id, has_side_effects=True, vmem_limit_bytes=40 * 1024 * 1024
        ),
    )(send, mask)


def from_owners(x, owners):
    if owners > 4:
        return [y for y in lax.all_gather(x, "adapter", axis=0)], jnp.arange(owners)
    parts = [x]
    for shift in range(1, owners):
        ring = [(i, (i + shift) % owners) for i in range(owners)]
        parts.append(lax.ppermute(x, "adapter", ring))
    return parts, lax.rem(lax.axis_index("adapter") - jnp.arange(owners) + owners, owners)


def i32(x):
    return x.astype(jnp.int32)


def shards(tokens, frozen_weight, down_tables, up_tables, cotangent, block_owner, block_region):
    lane_index = lax.axis_index(("tensor", "sub"))
    owners = lax.axis_size("adapter")
    me = lax.axis_index("adapter")
    group = lax.axis_index("groups")
    tok_rows, d_part = tokens.shape
    reg_dev, _, rank_width = down_tables.shape
    key_portion = up_tables.shape[2]
    blocks = tok_rows // BLOCK
    slot_limit = max(2, blocks // owners * 2)
    tables = jnp.swapaxes(down_tables, 1, 2)

    region = block_owner[:, 0] * reg_dev + block_region
    named = lax.all_gather(region, ("groups", "adapter"), axis=0, tiled=True)
    named = named.reshape(-1, owners, blocks)
    regions = owners * reg_dev
    present = i32(jnp.any(named[..., None] == jnp.arange(regions), axis=2))
    present = present.reshape(-1, owners, owners, reg_dev)
    counts = jnp.sum(present, axis=-1)
    apart = 1 - jnp.eye(owners, dtype=jnp.int32)
    need = jnp.max((counts + jnp.swapaxes(counts, 1, 2)) * apart)
    here = lax.dynamic_index_in_dim(present, group, 0, False)
    count = lax.dynamic_index_in_dim(counts, group, 0, False)
    before = jnp.arange(reg_dev)[:, None] < jnp.arange(reg_dev)[None, :]
    ranks = jnp.sum(here[..., :, None] * before, axis=-2)
    mine_in = lax.dynamic_index_in_dim(here, me, 0, False)
    mine_of = lax.dynamic_index_in_dim(here, me, 1, False)
    rank_in = lax.dynamic_index_in_dim(ranks, me, 0, False)
    rank_of = lax.dynamic_index_in_dim(ranks, me, 1, False)
    count_in = lax.dynamic_index_in_dim(count, me, 0, False)
    count_of = lax.dynamic_index_in_dim(count, me, 1, False)

    j = jnp.arange(blocks)
    less = region[:, None] < region[None, :]
    tie = (region[:, None] == region[None, :]) & (j[:, None] < j[None, :])
    place = jnp.sum(i32(less | tie), axis=0)
    order = jnp.sum(i32(place[:, None] == j[None, :]) * j[:, None], axis=0)
    first = jnp.sum(i32(less), axis=0)
    slot = jnp.sum(i32(place[:, None] == j[None, :]) * first[:, None], axis=0)
    term_slot = jnp.sum(i32(region[:, None] < jnp.arange(regions)[None, :]), axis=0)
    term_slot = jnp.minimum(term_slot, blocks - 1).reshape(owners, reg_dev)

    up_parts, up_place = from_owners(up_tables, owners)
    up_all = jnp.concatenate(up_parts, axis=0)
    up_at = jnp.sum(i32(block_owner == jnp.arange(owners)) * up_place, axis=1) * reg_dev + block_region
    up_part = up_down_parts(up_at, up_all, cotangent)
    low_up = lax.psum(up_part, ("tensor", "sub")).astype(jnp.float32)
    low_up = (adapter_scale * low_up).astype(jnp.bfloat16)
    terms = summed_terms(order, slot, low_up, tokens, 1.0)

    frozen_weight, up_all = lax.optimization_barrier((frozen_weight, up_all))
    weights, weight_place = from_owners(frozen_weight, owners)
    frozen_part = jnp.dot(
        tokens, jnp.concatenate(weights, axis=1), preferred_element_type=jnp.float32
    )
    frozen_sum = lax.psum_scatter(
        frozen_part.astype(jnp.bfloat16), ("tensor", "sub"), scatter_dimension=0, tiled=True
    )
    lanes = lax.axis_size("tensor") * lax.axis_size("sub")
    up_blocks = jnp.take(up_all, up_at, axis=0, mode="clip")
    up_wide = lax.all_to_all(
        up_blocks, ("tensor", "sub"), split_axis=0, concat_axis=2, tiled=True
    )

    def line_tracks(w):
        base = jnp.stack([
            jnp.stack([w[0, 0] * 0, w[0, 3] + w[0, 2], w[0, 3], w[0, 0] * 0]),
            jnp.stack([w[0, 3] + w[0, 2], w[0, 0] * 0, w[0, 3] + w[0, 2] + w[1, 3], w[0, 3] + w[0, 2]]),
            jnp.stack([w[0, 3], w[0, 3] + w[0, 2] + w[1, 3], w[0, 0] * 0, w[0, 3]]),
            jnp.stack([w[0, 0] * 0, w[0, 3] + w[0, 2], w[0, 3], w[0, 0] * 0]),
        ])
        row = lax.dynamic_index_in_dim(base, me, 0, False)
        jumps = (me + jnp.arange(owners) == 5)[:, None]

        def track(k):
            return row[:, None] + k + jnp.where(jumps & (k >= w[0, 2]), w[1, 3], 0)

        return track

    def line(index, tracks, tables, terms, tokens):
        track = line_tracks(count + count.T)
        t = jnp.arange(tracks)
        peer = jnp.arange(owners)
        table_track = track(rank_of)
        term_track = track(count_of[:, None] + rank_in)
        takes_table = mine_of[:, :, None] * i32(table_track[:, :, None] == t)
        takes_term = mine_in[:, :, None] * i32(term_track[:, :, None] == t)
        ways = jnp.stack([peer > me, peer < me])[:, :, None, None]
        takes_table = ways * takes_table
        takes_term = ways * takes_term
        table_at = jnp.sum(takes_table * jnp.arange(reg_dev)[:, None], axis=(1, 2)).reshape(-1)
        term_at = jnp.sum(takes_term * term_slot[:, :, None], axis=(1, 2)).reshape(-1)
        has_table = jnp.sum(takes_table, axis=(1, 2)).reshape(-1)
        has_term = jnp.sum(takes_term, axis=(1, 2)).reshape(-1)
        kind = i32(jnp.where(has_table > 0, 0, jnp.where(has_term > 0, 1, 2)))
        send = pack(table_at, term_at, kind, tables, terms)
        parts = 2
        mask = jnp.repeat(i32(kind < 2), parts)
        got = line_exchange(
            tracks * parts, index, send.reshape(2 * tracks * parts, rank_width // parts, d_part), mask
        ).reshape(2 * tracks, rank_width, d_part)
        side = jnp.where(peer < me, 0, tracks)[:, None]
        flat = (side + track(rank_in)).reshape(-1)
        own = i32(block_owner[:, 0] == me)
        got_at = jnp.sum(i32(region[:, None] == jnp.arange(regions)) * flat, axis=1) * (1 - own)
        inner = inner_parts(got_at, block_region * own, own, got, tables, tokens)
        remote = mine_of.T * (1 - i32(peer == me))
        back_at = (side + track(count_in[:, None] + rank_of)).T
        own_terms = lax.dynamic_index_in_dim(mine_in, me, 0, False)
        own_slots = lax.dynamic_index_in_dim(term_slot, me, 0, False)
        valid = jnp.concatenate([remote, own_terms[:, None]], axis=1)
        grad = owner_sum(back_at * remote, own_slots * own_terms, valid, got, terms, reg_dev)
        return inner, grad

    def exchange(slots, tables, terms, tokens):
        s = jnp.arange(slots)
        takes_table = mine_of[:, :, None] * i32(rank_of[:, :, None] == s)
        shifted = rank_in + count_of[:, None]
        takes_term = mine_in[:, :, None] * i32(shifted[:, :, None] == s)
        table_at = jnp.sum(takes_table * jnp.arange(reg_dev)[:, None], axis=1)
        term_at = jnp.sum(takes_term * term_slot[:, :, None], axis=1)
        other = i32(jnp.arange(owners) != me)[:, None]
        kind = jnp.where(
            other * jnp.sum(takes_table, axis=1) > 0,
            0,
            jnp.where(other * jnp.sum(takes_term, axis=1) > 0, 1, 2),
        )
        send = pack(table_at.reshape(-1), term_at.reshape(-1), i32(kind).reshape(-1), tables, terms)
        got = lax.all_to_all(
            send.reshape(owners, slots, rank_width, d_part),
            "adapter", split_axis=0, concat_axis=0, tiled=True,
        ).reshape(owners * slots, rank_width, d_part)
        flat = (jnp.arange(owners)[:, None] * slots + rank_in).reshape(-1)
        own = i32(block_owner[:, 0] == me)
        pick = i32(region[:, None] == jnp.arange(regions))
        got_at = jnp.sum(pick * flat, axis=1) * (1 - own)
        inner = inner_parts(got_at, block_region * own, own, got, tables, tokens)
        remote = mine_of.T * (1 - i32(jnp.arange(owners) == me))
        back_at = (jnp.arange(owners) * slots + count_in)[None, :] + rank_of.T
        own_terms = lax.dynamic_index_in_dim(mine_in, me, 0, False)
        own_slots = lax.dynamic_index_in_dim(term_slot, me, 0, False)
        valid = jnp.concatenate([remote, own_terms[:, None]], axis=1)
        grad = owner_sum(back_at * remote, own_slots * own_terms, valid, got, terms, reg_dev)
        return inner, grad

    if owners == 4:
        both = counts + jnp.swapaxes(counts, 1, 2)
        ids = jnp.arange(owners)
        loads = []
        for cut in range(owners - 1):
            over = i32((ids[:, None] <= cut) & (ids[None, :] > cut))
            loads.append(jnp.max(jnp.sum(both * over, axis=(1, 2))))
        need = jnp.max(jnp.stack(loads))
        full = blocks * owners
        sizes = sorted({-(-full * f // 64) for f in (26, 28, 30, 32, 38, 64)})
        bodies = [functools.partial(line, i, n) for i, n in enumerate(sizes)]
    else:
        full = 2 * slot_limit
        sizes = sorted({-(-full * f // 16) for f in (8, 10, 12, 16)})
        bodies = [functools.partial(exchange, n) for n in sizes]
    branch = jnp.sum(i32(need > jnp.array(sizes[:-1], jnp.int32)))
    inner, grad_down = lax.switch(branch, bodies, tables, terms, tokens)

    low_down = lax.psum(inner, ("tensor", "sub"))
    mine = tok_rows // lanes
    low_mine = lax.dynamic_slice_in_dim(low_down, lane_index * mine, mine, 1)
    low_mine = low_mine.reshape(rank_width, mine // BLOCK, BLOCK)
    lora = adapter_scale * jnp.einsum(
        "rbt,brk->btk", low_mine, up_wide, preferred_element_type=jnp.float32
    )
    width = frozen_weight.shape[1]
    frozen_sum = jnp.concatenate(
        [lax.dynamic_slice_in_dim(frozen_sum, weight_place[o] * width, width, 1) for o in range(owners)],
        axis=1,
    )
    projected = (frozen_sum.astype(jnp.float32) + lora.reshape(frozen_sum.shape)).astype(jnp.bfloat16)

    up_terms = summed_terms(order, slot, low_down, cotangent, adapter_scale)
    s = jnp.arange(slot_limit)
    takes = mine_in[:, :, None] * i32(rank_in[:, :, None] == s)
    term_at = jnp.sum(takes * term_slot[:, :, None], axis=1).reshape(-1)
    up_send = jnp.take(up_terms, term_at, axis=0, mode="clip")
    up_got = lax.all_to_all(
        up_send.reshape(owners, slot_limit, rank_width, key_portion),
        "adapter", split_axis=0, concat_axis=0, tiled=True,
    ).reshape(owners * slot_limit, rank_width, key_portion)
    back_at = (jnp.arange(owners) * slot_limit)[None, :] + jnp.minimum(rank_of.T, slot_limit - 1)
    valid = jnp.concatenate([mine_of.T, jnp.zeros((reg_dev, 1), jnp.int32)], axis=1)
    grad_up = owner_sum(
        back_at * mine_of.T, jnp.zeros((reg_dev,), jnp.int32), valid, up_got, up_got, reg_dev
    )
    return (projected, jnp.swapaxes(grad_down, 1, 2), grad_up)


def solution(mesh):
    return jax.shard_map(
        shards,
        mesh=mesh,
        in_specs=(
            P(("groups", "adapter"), ("tensor", "sub")),
            P(("tensor", "sub"), "adapter"),
            P("adapter", ("tensor", "sub"), None),
            P("adapter", None, ("tensor", "sub")),
            P(("groups", "adapter"), ("tensor", "sub")),
            P(("groups", "adapter"), None),
            P(("groups", "adapter")),
        ),
        out_specs=(
            P(("groups", "adapter", "tensor", "sub"), None),
            P(("groups", "adapter"), ("tensor", "sub"), None),
            P(("groups", "adapter"), None, ("tensor", "sub")),
        ),
        check_vma=False,
    )
```

```python
import functools

import jax
import jax.numpy as jnp
from jax import lax
from jax.experimental import pallas as pl
from jax.experimental.pallas import tpu as pltpu
from jax.sharding import PartitionSpec as P

BLOCK = 128


adapter_scale = 0.25

NT = (((1,), (1,)), ((), ()))
NN = (((1,), (0,)), ((), ()))
TN = (((0,), (0,)), ((), ()))


def dot(a, b, dims):
    return lax.dot_general(a, b, dims, preferred_element_type=jnp.float32)


def params():
    return pltpu.CompilerParams(vmem_limit_bytes=40 * 1024 * 1024)


def up_down_parts(region, up_all, cotangent):
    _, rank, cols = up_all.shape
    rows = cotangent.shape[0]

    def kernel(region_ref, up_ref, cot_ref, out_ref):
        out_ref[...] = dot(up_ref[0], cot_ref[...], NT).astype(out_ref.dtype)

    return pl.pallas_call(
        kernel,
        grid_spec=pltpu.PrefetchScalarGridSpec(
            num_scalar_prefetch=1,
            grid=(rows // BLOCK,),
            in_specs=[
                pl.BlockSpec((1, rank, cols), lambda i, r: (r[i], 0, 0)),
                pl.BlockSpec((BLOCK, cols), lambda i, r: (i, 0)),
            ],
            out_specs=pl.BlockSpec((rank, BLOCK), lambda i, r: (0, i)),
        ),
        out_shape=jax.ShapeDtypeStruct((rank, rows), jnp.bfloat16),
        compiler_params=params(),
    )(region, up_all, cotangent)


def summed_terms(order, slot, low, values, scale):
    rank = low.shape[0]
    rows, cols = values.shape
    blocks = rows // BLOCK

    def kernel(order_ref, slot_ref, low_ref, val_ref, out_ref, total):
        i = pl.program_id(0)
        part = dot(low_ref[...], val_ref[...], NN)
        fresh = slot_ref[i] == i

        @pl.when(fresh)
        def _():
            total[...] = part

        @pl.when(jnp.logical_not(fresh))
        def _():
            total[...] += part

        out_ref[0] = (total[...] * scale).astype(out_ref.dtype)

    return pl.pallas_call(
        kernel,
        grid_spec=pltpu.PrefetchScalarGridSpec(
            num_scalar_prefetch=2,
            grid=(blocks,),
            in_specs=[
                pl.BlockSpec((rank, BLOCK), lambda i, o, s: (0, o[i])),
                pl.BlockSpec((BLOCK, cols), lambda i, o, s: (o[i], 0)),
            ],
            out_specs=pl.BlockSpec((1, rank, cols), lambda i, o, s: (s[i], 0, 0)),
            scratch_shapes=[pltpu.VMEM((rank, cols), jnp.float32)],
        ),
        out_shape=jax.ShapeDtypeStruct((blocks, rank, cols), jnp.bfloat16),
        compiler_params=params(),
    )(order, slot, low, values)


def pack(table_at, term_at, kind, tables, terms):
    count = kind.shape[0]
    _, rank, cols = tables.shape

    def kernel(table_ref_at, term_ref_at, kind_ref, table_ref, term_ref, out_ref, sem):
        def start(i, carry):
            what = kind_ref[i]

            @pl.when(what == 0)
            def _():
                pltpu.make_async_copy(table_ref.at[table_ref_at[i]], out_ref.at[i], sem.at[i]).start()

            @pl.when(what == 1)
            def _():
                pltpu.make_async_copy(term_ref.at[term_ref_at[i]], out_ref.at[i], sem.at[i]).start()

            return carry

        def finish(i, carry):
            @pl.when(kind_ref[i] < 2)
            def _():
                pltpu.make_async_copy(table_ref.at[0], out_ref.at[i], sem.at[i]).wait()

            return carry

        lax.fori_loop(0, count, start, 0)
        lax.fori_loop(0, count, finish, 0)

    smem = pl.BlockSpec(memory_space=pltpu.SMEM)
    hbm = pl.BlockSpec(memory_space=pl.ANY)
    return pl.pallas_call(
        kernel,
        in_specs=[smem, smem, smem, hbm, hbm],
        out_specs=hbm,
        out_shape=jax.ShapeDtypeStruct((count, rank, cols), tables.dtype),
        scratch_shapes=[pltpu.SemaphoreType.DMA((count,))],
        compiler_params=params(),
    )(table_at, term_at, kind, tables, terms)


def inner_parts(got_at, own_at, own, got, tables, tokens):
    _, rank, cols = tables.shape
    rows = tokens.shape[0]

    def kernel(got_ref_at, own_ref_at, own_ref, got_ref, table_ref, tok_ref, out_ref):
        mine = own_ref[pl.program_id(0)] == 1

        @pl.when(mine)
        def _():
            out_ref[...] = dot(table_ref[0], tok_ref[...], NT).astype(out_ref.dtype)

        @pl.when(jnp.logical_not(mine))
        def _():
            out_ref[...] = dot(got_ref[0], tok_ref[...], NT).astype(out_ref.dtype)

    return pl.pallas_call(
        kernel,
        grid_spec=pltpu.PrefetchScalarGridSpec(
            num_scalar_prefetch=3,
            grid=(rows // BLOCK,),
            in_specs=[
                pl.BlockSpec((1, rank, cols), lambda i, g, t, o: (g[i], 0, 0)),
                pl.BlockSpec((1, rank, cols), lambda i, g, t, o: (t[i], 0, 0)),
                pl.BlockSpec((BLOCK, cols), lambda i, g, t, o: (i, 0)),
            ],
            out_specs=pl.BlockSpec((rank, BLOCK), lambda i, g, t, o: (0, i)),
        ),
        out_shape=jax.ShapeDtypeStruct((rank, rows), jnp.bfloat16),
        compiler_params=params(),
    )(got_at, own_at, own, got, tables, tokens)


def owner_sum(got_at, own_at, valid, got, terms, regions):
    consumers = valid.shape[1] - 1
    _, rank, cols = got.shape

    def kernel(got_ref_at, own_ref_at, valid_ref, *refs):
        i = pl.program_id(0)
        out_ref, total = refs[-2], refs[-1]
        total[...] = jnp.zeros_like(total)
        for c in range(consumers + 1):

            @pl.when(valid_ref[i, c] == 1)
            def _(c=c):
                total[...] += refs[c][0].astype(jnp.float32)

        out_ref[0] = total[...].astype(out_ref.dtype)

    def got_map(c, i, g, t, v):
        return (g[i, c], 0, 0)

    return pl.pallas_call(
        kernel,
        grid_spec=pltpu.PrefetchScalarGridSpec(
            num_scalar_prefetch=3,
            grid=(regions,),
            in_specs=[
                pl.BlockSpec((1, rank, cols), functools.partial(got_map, c))
                for c in range(consumers)
            ]
            + [pl.BlockSpec((1, rank, cols), lambda i, g, t, v: (t[i], 0, 0))],
            out_specs=pl.BlockSpec((1, rank, cols), lambda i, g, t, v: (i, 0, 0)),
            scratch_shapes=[pltpu.VMEM((rank, cols), jnp.float32)],
        ),
        out_shape=jax.ShapeDtypeStruct((regions, rank, cols), jnp.bfloat16),
        compiler_params=params(),
    )(got_at, own_at, valid, *([got] * consumers), terms)


def line_exchange(count, step_id, send, mask):
    total, rows, cols = send.shape
    lag, deep = 2, 3

    def kernel(send_ref, mask_ref, got_ref, own_buf, pass_buf, out_buf, load_sem, pass_sem, send_sem, recv_sem):
        me = lax.axis_index("adapter")
        last = lax.axis_size("adapter") - 1
        barrier = pltpu.get_barrier_semaphore()

        @pl.when(me > 0)
        def _():
            pl.semaphore_signal(barrier, inc=1, device_id={"adapter": me - 1}, device_id_type=pl.DeviceIdType.MESH)

        @pl.when(me < last)
        def _():
            pl.semaphore_signal(barrier, inc=1, device_id={"adapter": me + 1}, device_id_type=pl.DeviceIdType.MESH)

        inside = (me > 0) & (me < last)

        @pl.when(inside)
        def _():
            pl.semaphore_wait(barrier, 2)

        @pl.when(jnp.logical_not(inside))
        def _():
            pl.semaphore_wait(barrier, 1)

        def remote(way, t):
            peer = me + 1 if way == 0 else me - 1
            slot = lax.rem(t, deep)
            return pltpu.make_async_remote_copy(
                src_ref=out_buf.at[way, slot],
                dst_ref=got_ref.at[way * count + t],
                send_sem=send_sem.at[way, slot],
                recv_sem=recv_sem.at[way, t],
                device_id={"adapter": peer},
                device_id_type=pl.DeviceIdType.MESH,
            )

        def own_load(way, t):
            return pltpu.make_async_copy(send_ref.at[way * count + t], own_buf.at[way], load_sem.at[way])

        def pass_load(way, t):
            return pltpu.make_async_copy(got_ref.at[way * count + t], pass_buf.at[way], pass_sem.at[way])

        places = (me, last - me)

        def step(i, carry):
            at = [i - lag * place for place in places]
            live = [(t >= 0) & (t < count) for t in at]
            sends = [ok & (place < last) for ok, place in zip(live, places)]
            for way in (0, 1):

                @pl.when(sends[way])
                def _(way=way):
                    own_load(way, at[way]).start()

            for way in (0, 1):

                @pl.when(live[way] & (places[way] > 0))
                def _(way=way):
                    remote(way, at[way]).wait_recv()

                @pl.when(sends[way] & (places[way] > 0))
                def _(way=way):
                    pass_load(way, at[way]).start()

            for way in (0, 1):

                @pl.when(sends[way])
                def _(way=way):
                    t = at[way]
                    slot = lax.rem(t, deep)

                    @pl.when(t >= deep)
                    def _():
                        remote(way, t).wait_send()

                    own_load(way, t).wait()

                    @pl.when(places[way] == 0)
                    def _():
                        out_buf[way, slot] = own_buf[way]

                    @pl.when(places[way] > 0)
                    def _():
                        pass_load(way, t).wait()
                        mine = jnp.broadcast_to(mask_ref[way * count + t], (rows, cols)) > 0
                        out_buf[way, slot] = jnp.where(
                            mine, own_buf[way].astype(jnp.float32), pass_buf[way].astype(jnp.float32)
                        ).astype(out_buf.dtype)

                    remote(way, t).start()

            return carry

        lax.fori_loop(0, count + lag * last, step, 0)
        for way in (0, 1):
            for t in range(count - deep, count):

                @pl.when(places[way] < last)
                def _(way=way, t=t):
                    remote(way, t).wait_send()

    return pl.pallas_call(
        kernel,
        in_specs=[
            pl.BlockSpec(memory_space=pl.ANY),
            pl.BlockSpec(memory_space=pltpu.SMEM),
        ],
        out_specs=pl.BlockSpec(memory_space=pl.ANY),
        out_shape=jax.ShapeDtypeStruct((total, rows, cols), send.dtype),
        scratch_shapes=[
            pltpu.VMEM((2, rows, cols), send.dtype),
            pltpu.VMEM((2, rows, cols), send.dtype),
            pltpu.VMEM((2, deep, rows, cols), send.dtype),
            pltpu.SemaphoreType.DMA((2,)),
            pltpu.SemaphoreType.DMA((2,)),
            pltpu.SemaphoreType.DMA((2, deep)),
            pltpu.SemaphoreType.DMA((2, count)),
        ],
        compiler_params=pltpu.CompilerParams(
            collective_id=step_id, has_side_effects=True, vmem_limit_bytes=40 * 1024 * 1024
        ),
    )(send, mask)


def from_owners(x, owners):
    if owners > 4:
        return [y for y in lax.all_gather(x, "adapter", axis=0)], jnp.arange(owners)
    parts = [x]
    for shift in range(1, owners):
        ring = [(i, (i + shift) % owners) for i in range(owners)]
        parts.append(lax.ppermute(x, "adapter", ring))
    return parts, lax.rem(lax.axis_index("adapter") - jnp.arange(owners) + owners, owners)


def i32(x):
    return x.astype(jnp.int32)


def shards(tokens, frozen_weight, down_tables, up_tables, cotangent, block_owner, block_region):
    lane_index = lax.axis_index(("tensor", "sub"))
    owners = lax.axis_size("adapter")
    me = lax.axis_index("adapter")
    group = lax.axis_index("groups")
    tok_rows, d_part = tokens.shape
    reg_dev, _, rank_width = down_tables.shape
    key_portion = up_tables.shape[2]
    blocks = tok_rows // BLOCK
    slot_limit = max(2, blocks // owners * 2)
    tables = jnp.swapaxes(down_tables, 1, 2)

    region = block_owner[:, 0] * reg_dev + block_region
    j = jnp.arange(blocks)
    less = region[:, None] < region[None, :]
    tie = (region[:, None] == region[None, :]) & (j[:, None] < j[None, :])
    place = jnp.sum(i32(less | tie), axis=0)
    order = jnp.sum(i32(place[:, None] == j[None, :]) * j[:, None], axis=0)
    first = jnp.sum(i32(less), axis=0)
    slot = jnp.sum(i32(place[:, None] == j[None, :]) * first[:, None], axis=0)
    regions = owners * reg_dev
    term_slot = jnp.sum(i32(region[:, None] < jnp.arange(regions)[None, :]), axis=0)
    term_slot = jnp.minimum(term_slot, blocks - 1).reshape(owners, reg_dev)

    up_parts, up_place = from_owners(up_tables, owners)
    up_all = jnp.concatenate(up_parts, axis=0)
    up_at = jnp.sum(i32(block_owner == jnp.arange(owners)) * up_place, axis=1) * reg_dev + block_region
    up_part = up_down_parts(up_at, up_all, cotangent)
    up_part, late_region = lax.optimization_barrier((up_part, region))

    named = lax.all_gather(late_region, ("groups", "adapter"), axis=0, tiled=True)
    named = named.reshape(-1, owners, blocks)
    present = i32(jnp.any(named[..., None] == jnp.arange(regions), axis=2))
    present = present.reshape(-1, owners, owners, reg_dev)
    counts = jnp.sum(present, axis=-1)
    apart = 1 - jnp.eye(owners, dtype=jnp.int32)
    need = jnp.max((counts + jnp.swapaxes(counts, 1, 2)) * apart)
    here = lax.dynamic_index_in_dim(present, group, 0, False)
    count = lax.dynamic_index_in_dim(counts, group, 0, False)
    before = jnp.arange(reg_dev)[:, None] < jnp.arange(reg_dev)[None, :]
    ranks = jnp.sum(here[..., :, None] * before, axis=-2)
    mine_in = lax.dynamic_index_in_dim(here, me, 0, False)
    mine_of = lax.dynamic_index_in_dim(here, me, 1, False)
    rank_in = lax.dynamic_index_in_dim(ranks, me, 0, False)
    rank_of = lax.dynamic_index_in_dim(ranks, me, 1, False)
    count_in = lax.dynamic_index_in_dim(count, me, 0, False)
    count_of = lax.dynamic_index_in_dim(count, me, 1, False)

    low_up = lax.psum(up_part, ("tensor", "sub")).astype(jnp.float32)
    low_up = (adapter_scale * low_up).astype(jnp.bfloat16)
    terms = summed_terms(order, slot, low_up, tokens, 1.0)

    frozen_weight, up_all = lax.optimization_barrier((frozen_weight, up_all))
    weights, weight_place = from_owners(frozen_weight, owners)
    weight = jnp.concatenate(weights, axis=1)
    lanes = lax.axis_size("tensor") * lax.axis_size("sub")
    up_blocks = jnp.take(up_all, up_at, axis=0, mode="clip")
    up_wide = lax.all_to_all(
        up_blocks, ("tensor", "sub"), split_axis=0, concat_axis=2, tiled=True
    )

    def finish(inner, tokens, weight):
        low_down = lax.psum(inner, ("tensor", "sub"))
        frozen = jnp.dot(tokens, weight, preferred_element_type=jnp.float32)
        return low_down, frozen.astype(jnp.bfloat16)

    def line_tracks(w):
        base = jnp.stack([
            jnp.stack([w[0, 0] * 0, w[0, 3] + w[0, 2], w[0, 3], w[0, 0] * 0]),
            jnp.stack([w[0, 3] + w[0, 2], w[0, 0] * 0, w[0, 3] + w[0, 2] + w[1, 3], w[0, 3] + w[0, 2]]),
            jnp.stack([w[0, 3], w[0, 3] + w[0, 2] + w[1, 3], w[0, 0] * 0, w[0, 3]]),
            jnp.stack([w[0, 0] * 0, w[0, 3] + w[0, 2], w[0, 3], w[0, 0] * 0]),
        ])
        row = lax.dynamic_index_in_dim(base, me, 0, False)
        jumps = (me + jnp.arange(owners) == 5)[:, None]

        def track(k):
            return row[:, None] + k + jnp.where(jumps & (k >= w[0, 2]), w[1, 3], 0)

        return track

    def line(index, tracks, tables, terms, tokens, weight):
        track = line_tracks(count + count.T)
        t = jnp.arange(tracks)
        peer = jnp.arange(owners)
        table_track = track(rank_of)
        term_track = track(count_of[:, None] + rank_in)
        takes_table = mine_of[:, :, None] * i32(table_track[:, :, None] == t)
        takes_term = mine_in[:, :, None] * i32(term_track[:, :, None] == t)
        ways = jnp.stack([peer > me, peer < me])[:, :, None, None]
        takes_table = ways * takes_table
        takes_term = ways * takes_term
        table_at = jnp.sum(takes_table * jnp.arange(reg_dev)[:, None], axis=(1, 2)).reshape(-1)
        term_at = jnp.sum(takes_term * term_slot[:, :, None], axis=(1, 2)).reshape(-1)
        has_table = jnp.sum(takes_table, axis=(1, 2)).reshape(-1)
        has_term = jnp.sum(takes_term, axis=(1, 2)).reshape(-1)
        kind = i32(jnp.where(has_table > 0, 0, jnp.where(has_term > 0, 1, 2)))
        send = pack(table_at, term_at, kind, tables, terms)
        parts = 2
        mask = jnp.repeat(i32(kind < 2), parts)
        got = line_exchange(
            tracks * parts, index, send.reshape(2 * tracks * parts, rank_width // parts, d_part), mask
        ).reshape(2 * tracks, rank_width, d_part)
        side = jnp.where(peer < me, 0, tracks)[:, None]
        flat = (side + track(rank_in)).reshape(-1)
        own = i32(block_owner[:, 0] == me)
        got_at = jnp.sum(i32(region[:, None] == jnp.arange(regions)) * flat, axis=1) * (1 - own)
        inner = inner_parts(got_at, block_region * own, own, got, tables, tokens)
        remote = mine_of.T * (1 - i32(peer == me))
        back_at = (side + track(count_in[:, None] + rank_of)).T
        own_terms = lax.dynamic_index_in_dim(mine_in, me, 0, False)
        own_slots = lax.dynamic_index_in_dim(term_slot, me, 0, False)
        valid = jnp.concatenate([remote, own_terms[:, None]], axis=1)
        grad = owner_sum(back_at * remote, own_slots * own_terms, valid, got, terms, reg_dev)
        return finish(inner, tokens, weight), grad

    def exchange(slots, tables, terms, tokens, weight):
        s = jnp.arange(slots)
        takes_table = mine_of[:, :, None] * i32(rank_of[:, :, None] == s)
        shifted = rank_in + count_of[:, None]
        takes_term = mine_in[:, :, None] * i32(shifted[:, :, None] == s)
        table_at = jnp.sum(takes_table * jnp.arange(reg_dev)[:, None], axis=1)
        term_at = jnp.sum(takes_term * term_slot[:, :, None], axis=1)
        other = i32(jnp.arange(owners) != me)[:, None]
        kind = jnp.where(
            other * jnp.sum(takes_table, axis=1) > 0,
            0,
            jnp.where(other * jnp.sum(takes_term, axis=1) > 0, 1, 2),
        )
        send = pack(table_at.reshape(-1), term_at.reshape(-1), i32(kind).reshape(-1), tables, terms)
        got = lax.all_to_all(
            send.reshape(owners, slots, rank_width, d_part),
            "adapter", split_axis=0, concat_axis=0, tiled=True,
        ).reshape(owners * slots, rank_width, d_part)
        flat = (jnp.arange(owners)[:, None] * slots + rank_in).reshape(-1)
        own = i32(block_owner[:, 0] == me)
        pick = i32(region[:, None] == jnp.arange(regions))
        got_at = jnp.sum(pick * flat, axis=1) * (1 - own)
        inner = inner_parts(got_at, block_region * own, own, got, tables, tokens)
        remote = mine_of.T * (1 - i32(jnp.arange(owners) == me))
        back_at = (jnp.arange(owners) * slots + count_in)[None, :] + rank_of.T
        own_terms = lax.dynamic_index_in_dim(mine_in, me, 0, False)
        own_slots = lax.dynamic_index_in_dim(term_slot, me, 0, False)
        valid = jnp.concatenate([remote, own_terms[:, None]], axis=1)
        grad = owner_sum(back_at * remote, own_slots * own_terms, valid, got, terms, reg_dev)
        return finish(inner, tokens, weight), grad

    if owners == 4:
        both = counts + jnp.swapaxes(counts, 1, 2)
        ids = jnp.arange(owners)
        loads = []
        for cut in range(owners - 1):
            over = i32((ids[:, None] <= cut) & (ids[None, :] > cut))
            loads.append(jnp.max(jnp.sum(both * over, axis=(1, 2))))
        need = jnp.max(jnp.stack(loads))
        full = blocks * owners
        sizes = sorted({-(-full * f // 64) for f in (26, 27, 28, 29, 30, 32, 36, 64)})
        bodies = [functools.partial(line, i, n) for i, n in enumerate(sizes)]
    else:
        full = 2 * slot_limit
        sizes = sorted({-(-full * f // 16) for f in (8, 10, 12, 16)})
        bodies = [functools.partial(exchange, n) for n in sizes]
    branch = jnp.sum(i32(need > jnp.array(sizes[:-1], jnp.int32)))
    (low_down, frozen_part), grad_down = lax.switch(branch, bodies, tables, terms, tokens, weight)

    frozen_sum = lax.psum_scatter(
        frozen_part, ("tensor", "sub"), scatter_dimension=0, tiled=True
    )
    mine = tok_rows // lanes
    low_mine = lax.dynamic_slice_in_dim(low_down, lane_index * mine, mine, 1)
    low_mine = low_mine.reshape(rank_width, mine // BLOCK, BLOCK)
    lora = adapter_scale * jnp.einsum(
        "rbt,brk->btk", low_mine, up_wide, preferred_element_type=jnp.float32
    )
    width = frozen_weight.shape[1]
    frozen_sum = jnp.concatenate(
        [lax.dynamic_slice_in_dim(frozen_sum, weight_place[o] * width, width, 1) for o in range(owners)],
        axis=1,
    )
    projected = (frozen_sum.astype(jnp.float32) + lora.reshape(frozen_sum.shape)).astype(jnp.bfloat16)

    up_terms = summed_terms(order, slot, low_down, cotangent, adapter_scale)
    s = jnp.arange(slot_limit)
    takes = mine_in[:, :, None] * i32(rank_in[:, :, None] == s)
    term_at = jnp.sum(takes * term_slot[:, :, None], axis=1).reshape(-1)
    up_send = jnp.take(up_terms, term_at, axis=0, mode="clip")
    up_got = lax.all_to_all(
        up_send.reshape(owners, slot_limit, rank_width, key_portion),
        "adapter", split_axis=0, concat_axis=0, tiled=True,
    ).reshape(owners * slot_limit, rank_width, key_portion)
    back_at = (jnp.arange(owners) * slot_limit)[None, :] + jnp.minimum(rank_of.T, slot_limit - 1)
    valid = jnp.concatenate([mine_of.T, jnp.zeros((reg_dev, 1), jnp.int32)], axis=1)
    grad_up = owner_sum(
        back_at * mine_of.T, jnp.zeros((reg_dev,), jnp.int32), valid, up_got, up_got, reg_dev
    )
    return (projected, jnp.swapaxes(grad_down, 1, 2), grad_up)


def solution(mesh):
    return jax.shard_map(
        shards,
        mesh=mesh,
        in_specs=(
            P(("groups", "adapter"), ("tensor", "sub")),
            P(("tensor", "sub"), "adapter"),
            P("adapter", ("tensor", "sub"), None),
            P("adapter", None, ("tensor", "sub")),
            P(("groups", "adapter"), ("tensor", "sub")),
            P(("groups", "adapter"), None),
            P(("groups", "adapter")),
        ),
        out_specs=(
            P(("groups", "adapter", "tensor", "sub"), None),
            P(("groups", "adapter"), ("tensor", "sub"), None),
            P(("groups", "adapter"), None, ("tensor", "sub")),
        ),
        check_vma=False,
    )
```

```python
import functools

import jax
import jax.numpy as jnp
from jax import lax
from jax.experimental import pallas as pl
from jax.experimental.pallas import tpu as pltpu
from jax.sharding import PartitionSpec as P

BLOCK = 128


adapter_scale = 0.25

NT = (((1,), (1,)), ((), ()))
NN = (((1,), (0,)), ((), ()))
TN = (((0,), (0,)), ((), ()))


def dot(a, b, dims):
    return lax.dot_general(a, b, dims, preferred_element_type=jnp.float32)


def params():
    return pltpu.CompilerParams(vmem_limit_bytes=40 * 1024 * 1024)


def up_down_parts(region, up_all, cotangent):
    _, rank, cols = up_all.shape
    rows = cotangent.shape[0]

    def kernel(region_ref, up_ref, cot_ref, out_ref):
        out_ref[...] = dot(up_ref[0], cot_ref[...], NT).astype(out_ref.dtype)

    return pl.pallas_call(
        kernel,
        grid_spec=pltpu.PrefetchScalarGridSpec(
            num_scalar_prefetch=1,
            grid=(rows // BLOCK,),
            in_specs=[
                pl.BlockSpec((1, rank, cols), lambda i, r: (r[i], 0, 0)),
                pl.BlockSpec((BLOCK, cols), lambda i, r: (i, 0)),
            ],
            out_specs=pl.BlockSpec((rank, BLOCK), lambda i, r: (0, i)),
        ),
        out_shape=jax.ShapeDtypeStruct((rank, rows), jnp.bfloat16),
        compiler_params=params(),
    )(region, up_all, cotangent)


def summed_terms(order, slot, low, values, scale):
    rank = low.shape[0]
    rows, cols = values.shape
    blocks = rows // BLOCK

    def kernel(order_ref, slot_ref, low_ref, val_ref, out_ref, total):
        i = pl.program_id(0)
        part = dot(low_ref[...], val_ref[...], NN)
        fresh = slot_ref[i] == i

        @pl.when(fresh)
        def _():
            total[...] = part

        @pl.when(jnp.logical_not(fresh))
        def _():
            total[...] += part

        out_ref[0] = (total[...] * scale).astype(out_ref.dtype)

    return pl.pallas_call(
        kernel,
        grid_spec=pltpu.PrefetchScalarGridSpec(
            num_scalar_prefetch=2,
            grid=(blocks,),
            in_specs=[
                pl.BlockSpec((rank, BLOCK), lambda i, o, s: (0, o[i])),
                pl.BlockSpec((BLOCK, cols), lambda i, o, s: (o[i], 0)),
            ],
            out_specs=pl.BlockSpec((1, rank, cols), lambda i, o, s: (s[i], 0, 0)),
            scratch_shapes=[pltpu.VMEM((rank, cols), jnp.float32)],
        ),
        out_shape=jax.ShapeDtypeStruct((blocks, rank, cols), jnp.bfloat16),
        compiler_params=params(),
    )(order, slot, low, values)


def pack(table_at, term_at, kind, tables, terms):
    count = kind.shape[0]
    _, rank, cols = tables.shape

    def kernel(table_ref_at, term_ref_at, kind_ref, table_ref, term_ref, out_ref, sem):
        def start(i, carry):
            what = kind_ref[i]

            @pl.when(what == 0)
            def _():
                pltpu.make_async_copy(table_ref.at[table_ref_at[i]], out_ref.at[i], sem.at[i]).start()

            @pl.when(what == 1)
            def _():
                pltpu.make_async_copy(term_ref.at[term_ref_at[i]], out_ref.at[i], sem.at[i]).start()

            return carry

        def finish(i, carry):
            @pl.when(kind_ref[i] < 2)
            def _():
                pltpu.make_async_copy(table_ref.at[0], out_ref.at[i], sem.at[i]).wait()

            return carry

        lax.fori_loop(0, count, start, 0)
        lax.fori_loop(0, count, finish, 0)

    smem = pl.BlockSpec(memory_space=pltpu.SMEM)
    hbm = pl.BlockSpec(memory_space=pl.ANY)
    vmem = pl.BlockSpec(memory_space=pltpu.VMEM)
    return pl.pallas_call(
        kernel,
        in_specs=[smem, smem, smem, vmem, vmem],
        out_specs=hbm,
        out_shape=jax.ShapeDtypeStruct((count, rank, cols), tables.dtype),
        scratch_shapes=[pltpu.SemaphoreType.DMA((count,))],
        compiler_params=params(),
    )(table_at, term_at, kind, tables, terms)


def inner_parts(got_at, own_at, own, got, tables, tokens):
    _, rank, cols = tables.shape
    rows = tokens.shape[0]

    def kernel(got_ref_at, own_ref_at, own_ref, got_ref, table_ref, tok_ref, out_ref):
        mine = own_ref[pl.program_id(0)] == 1

        @pl.when(mine)
        def _():
            out_ref[...] = dot(table_ref[0], tok_ref[...], NT).astype(out_ref.dtype)

        @pl.when(jnp.logical_not(mine))
        def _():
            out_ref[...] = dot(got_ref[0], tok_ref[...], NT).astype(out_ref.dtype)

    return pl.pallas_call(
        kernel,
        grid_spec=pltpu.PrefetchScalarGridSpec(
            num_scalar_prefetch=3,
            grid=(rows // BLOCK,),
            in_specs=[
                pl.BlockSpec((1, rank, cols), lambda i, g, t, o: (g[i], 0, 0)),
                pl.BlockSpec((1, rank, cols), lambda i, g, t, o: (t[i], 0, 0)),
                pl.BlockSpec((BLOCK, cols), lambda i, g, t, o: (i, 0)),
            ],
            out_specs=pl.BlockSpec((rank, BLOCK), lambda i, g, t, o: (0, i)),
        ),
        out_shape=jax.ShapeDtypeStruct((rank, rows), jnp.bfloat16),
        compiler_params=params(),
    )(got_at, own_at, own, got, tables, tokens)


def owner_sum(got_at, own_at, valid, got, terms, regions):
    consumers = valid.shape[1] - 1
    _, rank, cols = got.shape

    def kernel(got_ref_at, own_ref_at, valid_ref, *refs):
        i = pl.program_id(0)
        out_ref, total = refs[-2], refs[-1]
        total[...] = jnp.zeros_like(total)
        for c in range(consumers + 1):

            @pl.when(valid_ref[i, c] == 1)
            def _(c=c):
                total[...] += refs[c][0].astype(jnp.float32)

        out_ref[0] = total[...].astype(out_ref.dtype)

    def got_map(c, i, g, t, v):
        return (g[i, c], 0, 0)

    return pl.pallas_call(
        kernel,
        grid_spec=pltpu.PrefetchScalarGridSpec(
            num_scalar_prefetch=3,
            grid=(regions,),
            in_specs=[
                pl.BlockSpec((1, rank, cols), functools.partial(got_map, c))
                for c in range(consumers)
            ]
            + [pl.BlockSpec((1, rank, cols), lambda i, g, t, v: (t[i], 0, 0))],
            out_specs=pl.BlockSpec((1, rank, cols), lambda i, g, t, v: (i, 0, 0)),
            scratch_shapes=[pltpu.VMEM((rank, cols), jnp.float32)],
        ),
        out_shape=jax.ShapeDtypeStruct((regions, rank, cols), jnp.bfloat16),
        compiler_params=params(),
    )(got_at, own_at, valid, *([got] * consumers), terms)


def line_exchange(count, step_id, room, send, mask):
    _, rows, cols = send.shape
    lag, deep = 2, 3

    def kernel(send_ref, mask_ref, got_ref, own_buf, pass_buf, out_buf, load_sem, pass_sem, send_sem, recv_sem):
        me = lax.axis_index("adapter")
        last = lax.axis_size("adapter") - 1
        barrier = pltpu.get_barrier_semaphore()

        @pl.when(me > 0)
        def _():
            pl.semaphore_signal(barrier, inc=1, device_id={"adapter": me - 1}, device_id_type=pl.DeviceIdType.MESH)

        @pl.when(me < last)
        def _():
            pl.semaphore_signal(barrier, inc=1, device_id={"adapter": me + 1}, device_id_type=pl.DeviceIdType.MESH)

        inside = (me > 0) & (me < last)

        @pl.when(inside)
        def _():
            pl.semaphore_wait(barrier, 2)

        @pl.when(jnp.logical_not(inside))
        def _():
            pl.semaphore_wait(barrier, 1)

        def remote(way, t):
            peer = me + 1 if way == 0 else me - 1
            slot = lax.rem(t, deep)
            return pltpu.make_async_remote_copy(
                src_ref=out_buf.at[way, slot],
                dst_ref=got_ref.at[way * room + t],
                send_sem=send_sem.at[way, slot],
                recv_sem=recv_sem.at[way, t],
                device_id={"adapter": peer},
                device_id_type=pl.DeviceIdType.MESH,
            )

        def own_load(way, t):
            return pltpu.make_async_copy(send_ref.at[way * count + t], own_buf.at[way], load_sem.at[way])

        def pass_load(way, t):
            return pltpu.make_async_copy(got_ref.at[way * room + t], pass_buf.at[way], pass_sem.at[way])

        places = (me, last - me)

        def step(i, carry):
            at = [i - lag * place for place in places]
            live = [(t >= 0) & (t < count) for t in at]
            sends = [ok & (place < last) for ok, place in zip(live, places)]
            for way in (0, 1):

                @pl.when(sends[way])
                def _(way=way):
                    own_load(way, at[way]).start()

            for way in (0, 1):

                @pl.when(live[way] & (places[way] > 0))
                def _(way=way):
                    remote(way, at[way]).wait_recv()

                @pl.when(sends[way] & (places[way] > 0))
                def _(way=way):
                    pass_load(way, at[way]).start()

            for way in (0, 1):

                @pl.when(sends[way])
                def _(way=way):
                    t = at[way]
                    slot = lax.rem(t, deep)

                    @pl.when(t >= deep)
                    def _():
                        remote(way, t).wait_send()

                    own_load(way, t).wait()

                    @pl.when(places[way] == 0)
                    def _():
                        out_buf[way, slot] = own_buf[way]

                    @pl.when(places[way] > 0)
                    def _():
                        pass_load(way, t).wait()
                        mine = jnp.broadcast_to(mask_ref[way * count + t], (rows, cols)) > 0
                        out_buf[way, slot] = jnp.where(
                            mine, own_buf[way].astype(jnp.float32), pass_buf[way].astype(jnp.float32)
                        ).astype(out_buf.dtype)

                    remote(way, t).start()

            return carry

        lax.fori_loop(0, count + lag * last, step, 0)
        for way in (0, 1):
            for t in range(count - deep, count):

                @pl.when(places[way] < last)
                def _(way=way, t=t):
                    remote(way, t).wait_send()

    return pl.pallas_call(
        kernel,
        in_specs=[
            pl.BlockSpec(memory_space=pl.ANY),
            pl.BlockSpec(memory_space=pltpu.SMEM),
        ],
        out_specs=pl.BlockSpec(memory_space=pl.ANY),
        out_shape=jax.ShapeDtypeStruct((2 * room, rows, cols), send.dtype),
        scratch_shapes=[
            pltpu.VMEM((2, rows, cols), send.dtype),
            pltpu.VMEM((2, rows, cols), send.dtype),
            pltpu.VMEM((2, deep, rows, cols), send.dtype),
            pltpu.SemaphoreType.DMA((2,)),
            pltpu.SemaphoreType.DMA((2,)),
            pltpu.SemaphoreType.DMA((2, deep)),
            pltpu.SemaphoreType.DMA((2, count)),
        ],
        compiler_params=pltpu.CompilerParams(
            collective_id=step_id, has_side_effects=True, vmem_limit_bytes=40 * 1024 * 1024
        ),
    )(send, mask)


def from_owners(x, owners):
    if owners > 4:
        return [y for y in lax.all_gather(x, "adapter", axis=0)], jnp.arange(owners)
    parts = [x]
    for shift in range(1, owners):
        ring = [(i, (i + shift) % owners) for i in range(owners)]
        parts.append(lax.ppermute(x, "adapter", ring))
    return parts, lax.rem(lax.axis_index("adapter") - jnp.arange(owners) + owners, owners)


def i32(x):
    return x.astype(jnp.int32)


def shards(tokens, frozen_weight, down_tables, up_tables, cotangent, block_owner, block_region):
    lane_index = lax.axis_index(("tensor", "sub"))
    owners = lax.axis_size("adapter")
    me = lax.axis_index("adapter")
    group = lax.axis_index("groups")
    tok_rows, d_part = tokens.shape
    reg_dev, _, rank_width = down_tables.shape
    key_portion = up_tables.shape[2]
    blocks = tok_rows // BLOCK
    slot_limit = max(2, blocks // owners * 2)
    tables = jnp.swapaxes(down_tables, 1, 2)

    region = block_owner[:, 0] * reg_dev + block_region
    named = lax.all_gather(region, ("groups", "adapter"), axis=0, tiled=True)
    named = named.reshape(-1, owners, blocks)
    named, up_tables = lax.optimization_barrier((named, up_tables))
    regions = owners * reg_dev
    present = i32(jnp.any(named[..., None] == jnp.arange(regions), axis=2))
    present = present.reshape(-1, owners, owners, reg_dev)
    counts = jnp.sum(present, axis=-1)
    apart = 1 - jnp.eye(owners, dtype=jnp.int32)
    need = jnp.max((counts + jnp.swapaxes(counts, 1, 2)) * apart)
    here = lax.dynamic_index_in_dim(present, group, 0, False)
    count = lax.dynamic_index_in_dim(counts, group, 0, False)
    before = jnp.arange(reg_dev)[:, None] < jnp.arange(reg_dev)[None, :]
    ranks = jnp.sum(here[..., :, None] * before, axis=-2)
    mine_in = lax.dynamic_index_in_dim(here, me, 0, False)
    mine_of = lax.dynamic_index_in_dim(here, me, 1, False)
    rank_in = lax.dynamic_index_in_dim(ranks, me, 0, False)
    rank_of = lax.dynamic_index_in_dim(ranks, me, 1, False)
    count_in = lax.dynamic_index_in_dim(count, me, 0, False)
    count_of = lax.dynamic_index_in_dim(count, me, 1, False)

    j = jnp.arange(blocks)
    less = region[:, None] < region[None, :]
    tie = (region[:, None] == region[None, :]) & (j[:, None] < j[None, :])
    place = jnp.sum(i32(less | tie), axis=0)
    order = jnp.sum(i32(place[:, None] == j[None, :]) * j[:, None], axis=0)
    first = jnp.sum(i32(less), axis=0)
    slot = jnp.sum(i32(place[:, None] == j[None, :]) * first[:, None], axis=0)
    term_slot = jnp.sum(i32(region[:, None] < jnp.arange(regions)[None, :]), axis=0)
    term_slot = jnp.minimum(term_slot, blocks - 1).reshape(owners, reg_dev)

    up_parts, up_place = from_owners(up_tables, owners)
    up_all = jnp.concatenate(up_parts, axis=0)
    up_at = jnp.sum(i32(block_owner == jnp.arange(owners)) * up_place, axis=1) * reg_dev + block_region
    up_part = up_down_parts(up_at, up_all, cotangent)
    low_up = lax.psum(up_part, ("tensor", "sub")).astype(jnp.float32)
    low_up = (adapter_scale * low_up).astype(jnp.bfloat16)
    terms = summed_terms(order, slot, low_up, tokens, 1.0)

    frozen_weight, up_all = lax.optimization_barrier((frozen_weight, up_all))
    weights, weight_place = from_owners(frozen_weight, owners)
    weight = jnp.concatenate(weights, axis=1)
    lanes = lax.axis_size("tensor") * lax.axis_size("sub")
    up_blocks = jnp.take(up_all, up_at, axis=0, mode="clip")
    up_wide = lax.all_to_all(
        up_blocks, ("tensor", "sub"), split_axis=0, concat_axis=2, tiled=True
    )

    def line_tracks(w):
        base = jnp.stack([
            jnp.stack([w[0, 0] * 0, w[0, 3] + w[0, 2], w[0, 3], w[0, 0] * 0]),
            jnp.stack([w[0, 3] + w[0, 2], w[0, 0] * 0, w[0, 3] + w[0, 2] + w[1, 3], w[0, 3] + w[0, 2]]),
            jnp.stack([w[0, 3], w[0, 3] + w[0, 2] + w[1, 3], w[0, 0] * 0, w[0, 3]]),
            jnp.stack([w[0, 0] * 0, w[0, 3] + w[0, 2], w[0, 3], w[0, 0] * 0]),
        ])
        row = lax.dynamic_index_in_dim(base, me, 0, False)
        jumps = (me + jnp.arange(owners) == 5)[:, None]

        def track(k):
            return row[:, None] + k + jnp.where(jumps & (k >= w[0, 2]), w[1, 3], 0)

        return track

    peer = jnp.arange(owners)
    if owners == 4:
        full = blocks * owners
        sizes = sorted({-(-full * f // 64) for f in (26, 27, 28, 29, 30, 32, 36, 64)})
        both = counts + jnp.swapaxes(counts, 1, 2)
        loads = []
        for cut in range(owners - 1):
            over = i32((peer[:, None] <= cut) & (peer[None, :] > cut))
            loads.append(jnp.max(jnp.sum(both * over, axis=(1, 2))))
        need = jnp.max(jnp.stack(loads))
        track = line_tracks(count + count.T)
        ways = jnp.stack([peer > me, peer < me])
        side = jnp.where(peer < me, 0, full)[:, None]
    else:
        full = 2 * slot_limit
        sizes = sorted({-(-full * f // 16) for f in (8, 10, 12, 16)})
        ways = jnp.eye(owners, dtype=jnp.int32) * i32(peer != me)
        side = (peer * full)[:, None]

        def track(k):
            return k

    t = jnp.arange(full)
    takes_table = mine_of[:, :, None] * i32(track(rank_of)[:, :, None] == t)
    takes_term = mine_in[:, :, None] * i32(track(count_of[:, None] + rank_in)[:, :, None] == t)
    takes_table = i32(ways)[:, :, None, None] * takes_table
    takes_term = i32(ways)[:, :, None, None] * takes_term
    table_at = jnp.sum(takes_table * jnp.arange(reg_dev)[:, None], axis=(1, 2))
    term_at = jnp.sum(takes_term * term_slot[:, :, None], axis=(1, 2))
    has_table = jnp.sum(takes_table, axis=(1, 2))
    has_term = jnp.sum(takes_term, axis=(1, 2))
    kind = i32(jnp.where(has_table > 0, 0, jnp.where(has_term > 0, 1, 2)))
    branch = jnp.sum(i32(need > jnp.array(sizes[:-1], jnp.int32)))

    def exchange(index, tracks, table_at, term_at, kind, tables, terms):
        table_at, term_at, kind = [x[:, :tracks].reshape(-1) for x in (table_at, term_at, kind)]
        send = pack(table_at, term_at, kind, tables, terms)
        if owners == 4:
            parts = 2
            mask = jnp.repeat(i32(kind < 2), parts)
            send = send.reshape(2 * tracks * parts, rank_width // parts, d_part)
            got = line_exchange(tracks * parts, index, full * parts, send, mask)
            return got.reshape(2 * full, rank_width, d_part)
        got = lax.all_to_all(
            send.reshape(owners, tracks, rank_width, d_part),
            "adapter", split_axis=0, concat_axis=0, tiled=True,
        )
        got = jnp.pad(got, ((0, 0), (0, full - tracks), (0, 0), (0, 0)))
        return got.reshape(owners * full, rank_width, d_part)

    bodies = [functools.partial(exchange, i, n) for i, n in enumerate(sizes)]
    got = lax.switch(branch, bodies, table_at, term_at, kind, tables, terms)

    flat = (side + track(rank_in)).reshape(-1)
    own = i32(block_owner[:, 0] == me)
    got_at = jnp.sum(i32(region[:, None] == jnp.arange(regions)) * flat, axis=1) * (1 - own)
    remote = mine_of.T * (1 - i32(peer == me))
    back_at = (side + track(count_in[:, None] + rank_of)).T
    own_terms = lax.dynamic_index_in_dim(mine_in, me, 0, False)
    own_slots = lax.dynamic_index_in_dim(term_slot, me, 0, False)
    valid = jnp.concatenate([remote, own_terms[:, None]], axis=1)
    inner = inner_parts(got_at, block_region * own, own, got, tables, tokens)
    low_down = lax.psum(inner, ("tensor", "sub"))
    grad_down = owner_sum(back_at * remote, own_slots * own_terms, valid, got, terms, reg_dev)
    frozen_part = jnp.dot(tokens, weight, preferred_element_type=jnp.float32).astype(jnp.bfloat16)

    frozen_sum = lax.psum_scatter(
        frozen_part, ("tensor", "sub"), scatter_dimension=0, tiled=True
    )
    mine = tok_rows // lanes
    low_mine = lax.dynamic_slice_in_dim(low_down, lane_index * mine, mine, 1)
    low_mine = low_mine.reshape(rank_width, mine // BLOCK, BLOCK)
    lora = adapter_scale * jnp.einsum(
        "rbt,brk->btk", low_mine, up_wide, preferred_element_type=jnp.float32
    )
    width = frozen_weight.shape[1]
    frozen_sum = jnp.concatenate(
        [lax.dynamic_slice_in_dim(frozen_sum, weight_place[o] * width, width, 1) for o in range(owners)],
        axis=1,
    )
    projected = (frozen_sum.astype(jnp.float32) + lora.reshape(frozen_sum.shape)).astype(jnp.bfloat16)

    up_terms = summed_terms(order, slot, low_down, cotangent, adapter_scale)
    s = jnp.arange(slot_limit)
    takes = mine_in[:, :, None] * i32(rank_in[:, :, None] == s)
    term_at = jnp.sum(takes * term_slot[:, :, None], axis=1).reshape(-1)
    up_send = jnp.take(up_terms, term_at, axis=0, mode="clip")
    up_got = lax.all_to_all(
        up_send.reshape(owners, slot_limit, rank_width, key_portion),
        "adapter", split_axis=0, concat_axis=0, tiled=True,
    ).reshape(owners * slot_limit, rank_width, key_portion)
    back_at = (jnp.arange(owners) * slot_limit)[None, :] + jnp.minimum(rank_of.T, slot_limit - 1)
    valid = jnp.concatenate([mine_of.T, jnp.zeros((reg_dev, 1), jnp.int32)], axis=1)
    grad_up = owner_sum(
        back_at * mine_of.T, jnp.zeros((reg_dev,), jnp.int32), valid, up_got, up_got, reg_dev
    )
    return (projected, jnp.swapaxes(grad_down, 1, 2), grad_up)


def solution(mesh):
    return jax.shard_map(
        shards,
        mesh=mesh,
        in_specs=(
            P(("groups", "adapter"), ("tensor", "sub")),
            P(("tensor", "sub"), "adapter"),
            P("adapter", ("tensor", "sub"), None),
            P("adapter", None, ("tensor", "sub")),
            P(("groups", "adapter"), ("tensor", "sub")),
            P(("groups", "adapter"), None),
            P(("groups", "adapter")),
        ),
        out_specs=(
            P(("groups", "adapter", "tensor", "sub"), None),
            P(("groups", "adapter"), ("tensor", "sub"), None),
            P(("groups", "adapter"), None, ("tensor", "sub")),
        ),
        check_vma=False,
    )
```

```python
import functools

import jax
import jax.numpy as jnp
from jax import lax
from jax.experimental import pallas as pl
from jax.experimental.pallas import tpu as pltpu
from jax.sharding import PartitionSpec as P

BLOCK = 128


adapter_scale = 0.25

NT = (((1,), (1,)), ((), ()))
NN = (((1,), (0,)), ((), ()))
TN = (((0,), (0,)), ((), ()))


def dot(a, b, dims):
    return lax.dot_general(a, b, dims, preferred_element_type=jnp.float32)


def params():
    return pltpu.CompilerParams(vmem_limit_bytes=40 * 1024 * 1024)


def up_down_parts(region, up_all, cotangent):
    _, rank, cols = up_all.shape
    rows = cotangent.shape[0]

    def kernel(region_ref, up_ref, cot_ref, out_ref):
        out_ref[...] = dot(up_ref[0], cot_ref[...], NT).astype(out_ref.dtype)

    return pl.pallas_call(
        kernel,
        grid_spec=pltpu.PrefetchScalarGridSpec(
            num_scalar_prefetch=1,
            grid=(rows // BLOCK,),
            in_specs=[
                pl.BlockSpec((1, rank, cols), lambda i, r: (r[i], 0, 0)),
                pl.BlockSpec((BLOCK, cols), lambda i, r: (i, 0)),
            ],
            out_specs=pl.BlockSpec((rank, BLOCK), lambda i, r: (0, i)),
        ),
        out_shape=jax.ShapeDtypeStruct((rank, rows), jnp.bfloat16),
        compiler_params=params(),
    )(region, up_all, cotangent)


def summed_terms(order, slot, low, values, scale):
    rank = low.shape[0]
    rows, cols = values.shape
    blocks = rows // BLOCK

    def kernel(order_ref, slot_ref, low_ref, val_ref, out_ref, total):
        i = pl.program_id(0)
        part = dot(low_ref[...], val_ref[...], NN)
        fresh = slot_ref[i] == i

        @pl.when(fresh)
        def _():
            total[...] = part

        @pl.when(jnp.logical_not(fresh))
        def _():
            total[...] += part

        out_ref[0] = (total[...] * scale).astype(out_ref.dtype)

    return pl.pallas_call(
        kernel,
        grid_spec=pltpu.PrefetchScalarGridSpec(
            num_scalar_prefetch=2,
            grid=(blocks,),
            in_specs=[
                pl.BlockSpec((rank, BLOCK), lambda i, o, s: (0, o[i])),
                pl.BlockSpec((BLOCK, cols), lambda i, o, s: (o[i], 0)),
            ],
            out_specs=pl.BlockSpec((1, rank, cols), lambda i, o, s: (s[i], 0, 0)),
            scratch_shapes=[pltpu.VMEM((rank, cols), jnp.float32)],
        ),
        out_shape=jax.ShapeDtypeStruct((blocks, rank, cols), jnp.bfloat16),
        compiler_params=params(),
    )(order, slot, low, values)


def pack(table_at, term_at, kind, tables, terms):
    count = kind.shape[0]
    _, rank, cols = tables.shape

    def kernel(table_ref_at, term_ref_at, kind_ref, table_ref, term_ref, out_ref, sem):
        def start(i, carry):
            what = kind_ref[i]

            @pl.when(what == 0)
            def _():
                pltpu.make_async_copy(table_ref.at[table_ref_at[i]], out_ref.at[i], sem.at[i]).start()

            @pl.when(what == 1)
            def _():
                pltpu.make_async_copy(term_ref.at[term_ref_at[i]], out_ref.at[i], sem.at[i]).start()

            return carry

        def finish(i, carry):
            @pl.when(kind_ref[i] < 2)
            def _():
                pltpu.make_async_copy(table_ref.at[0], out_ref.at[i], sem.at[i]).wait()

            return carry

        lax.fori_loop(0, count, start, 0)
        lax.fori_loop(0, count, finish, 0)

    smem = pl.BlockSpec(memory_space=pltpu.SMEM)
    hbm = pl.BlockSpec(memory_space=pl.ANY)
    vmem = pl.BlockSpec(memory_space=pltpu.VMEM)
    return pl.pallas_call(
        kernel,
        in_specs=[smem, smem, smem, vmem, vmem],
        out_specs=hbm,
        out_shape=jax.ShapeDtypeStruct((count, rank, cols), tables.dtype),
        scratch_shapes=[pltpu.SemaphoreType.DMA((count,))],
        compiler_params=params(),
    )(table_at, term_at, kind, tables, terms)


def inner_parts(got_at, own_at, own, got, tables, tokens):
    _, rank, cols = tables.shape
    rows = tokens.shape[0]

    def kernel(got_ref_at, own_ref_at, own_ref, got_ref, table_ref, tok_ref, out_ref):
        mine = own_ref[pl.program_id(0)] == 1

        @pl.when(mine)
        def _():
            out_ref[...] = dot(table_ref[0], tok_ref[...], NT).astype(out_ref.dtype)

        @pl.when(jnp.logical_not(mine))
        def _():
            out_ref[...] = dot(got_ref[0], tok_ref[...], NT).astype(out_ref.dtype)

    return pl.pallas_call(
        kernel,
        grid_spec=pltpu.PrefetchScalarGridSpec(
            num_scalar_prefetch=3,
            grid=(rows // BLOCK,),
            in_specs=[
                pl.BlockSpec((1, rank, cols), lambda i, g, t, o: (g[i], 0, 0)),
                pl.BlockSpec((1, rank, cols), lambda i, g, t, o: (t[i], 0, 0)),
                pl.BlockSpec((BLOCK, cols), lambda i, g, t, o: (i, 0)),
            ],
            out_specs=pl.BlockSpec((rank, BLOCK), lambda i, g, t, o: (0, i)),
        ),
        out_shape=jax.ShapeDtypeStruct((rank, rows), jnp.bfloat16),
        compiler_params=params(),
    )(got_at, own_at, own, got, tables, tokens)


def owner_sum(got_at, own_at, valid, got, terms, regions):
    consumers = valid.shape[1] - 1
    _, rank, cols = got.shape

    def kernel(got_ref_at, own_ref_at, valid_ref, *refs):
        i = pl.program_id(0)
        out_ref, total = refs[-2], refs[-1]
        total[...] = jnp.zeros_like(total)
        for c in range(consumers + 1):

            @pl.when(valid_ref[i, c] == 1)
            def _(c=c):
                total[...] += refs[c][0].astype(jnp.float32)

        out_ref[0] = total[...].astype(out_ref.dtype)

    def got_map(c, i, g, t, v):
        return (g[i, c], 0, 0)

    return pl.pallas_call(
        kernel,
        grid_spec=pltpu.PrefetchScalarGridSpec(
            num_scalar_prefetch=3,
            grid=(regions,),
            in_specs=[
                pl.BlockSpec((1, rank, cols), functools.partial(got_map, c))
                for c in range(consumers)
            ]
            + [pl.BlockSpec((1, rank, cols), lambda i, g, t, v: (t[i], 0, 0))],
            out_specs=pl.BlockSpec((1, rank, cols), lambda i, g, t, v: (i, 0, 0)),
            scratch_shapes=[pltpu.VMEM((rank, cols), jnp.float32)],
        ),
        out_shape=jax.ShapeDtypeStruct((regions, rank, cols), jnp.bfloat16),
        compiler_params=params(),
    )(got_at, own_at, valid, *([got] * consumers), terms)


def line_exchange(count, step_id, room, send, mask):
    _, rows, cols = send.shape
    lag, deep = 2, 3

    def kernel(send_ref, mask_ref, got_ref, own_buf, pass_buf, out_buf, load_sem, pass_sem, send_sem, recv_sem):
        me = lax.axis_index("adapter")
        last = lax.axis_size("adapter") - 1
        barrier = pltpu.get_barrier_semaphore()

        @pl.when(me > 0)
        def _():
            pl.semaphore_signal(barrier, inc=1, device_id={"adapter": me - 1}, device_id_type=pl.DeviceIdType.MESH)

        @pl.when(me < last)
        def _():
            pl.semaphore_signal(barrier, inc=1, device_id={"adapter": me + 1}, device_id_type=pl.DeviceIdType.MESH)

        inside = (me > 0) & (me < last)

        @pl.when(inside)
        def _():
            pl.semaphore_wait(barrier, 2)

        @pl.when(jnp.logical_not(inside))
        def _():
            pl.semaphore_wait(barrier, 1)

        def remote(way, t):
            peer = me + 1 if way == 0 else me - 1
            slot = lax.rem(t, deep)
            return pltpu.make_async_remote_copy(
                src_ref=out_buf.at[way, slot],
                dst_ref=got_ref.at[way * room + t],
                send_sem=send_sem.at[way, slot],
                recv_sem=recv_sem.at[way, t],
                device_id={"adapter": peer},
                device_id_type=pl.DeviceIdType.MESH,
            )

        def own_load(way, t):
            return pltpu.make_async_copy(send_ref.at[way * count + t], own_buf.at[way], load_sem.at[way])

        def pass_load(way, t):
            return pltpu.make_async_copy(got_ref.at[way * room + t], pass_buf.at[way], pass_sem.at[way])

        places = (me, last - me)

        def step(i, carry):
            at = [i - lag * place for place in places]
            live = [(t >= 0) & (t < count) for t in at]
            sends = [ok & (place < last) for ok, place in zip(live, places)]
            for way in (0, 1):

                @pl.when(sends[way])
                def _(way=way):
                    own_load(way, at[way]).start()

            for way in (0, 1):

                @pl.when(live[way] & (places[way] > 0))
                def _(way=way):
                    remote(way, at[way]).wait_recv()

                @pl.when(sends[way] & (places[way] > 0))
                def _(way=way):
                    pass_load(way, at[way]).start()

            for way in (0, 1):

                @pl.when(sends[way])
                def _(way=way):
                    t = at[way]
                    slot = lax.rem(t, deep)

                    @pl.when(t >= deep)
                    def _():
                        remote(way, t).wait_send()

                    own_load(way, t).wait()

                    @pl.when(places[way] == 0)
                    def _():
                        out_buf[way, slot] = own_buf[way]

                    @pl.when(places[way] > 0)
                    def _():
                        pass_load(way, t).wait()
                        mine = jnp.broadcast_to(mask_ref[way * count + t], (rows, cols)) > 0
                        out_buf[way, slot] = jnp.where(
                            mine, own_buf[way].astype(jnp.float32), pass_buf[way].astype(jnp.float32)
                        ).astype(out_buf.dtype)

                    remote(way, t).start()

            return carry

        lax.fori_loop(0, count + lag * last, step, 0)
        for way in (0, 1):
            for t in range(count - deep, count):

                @pl.when(places[way] < last)
                def _(way=way, t=t):
                    remote(way, t).wait_send()

    return pl.pallas_call(
        kernel,
        in_specs=[
            pl.BlockSpec(memory_space=pl.ANY),
            pl.BlockSpec(memory_space=pltpu.SMEM),
        ],
        out_specs=pl.BlockSpec(memory_space=pl.ANY),
        out_shape=jax.ShapeDtypeStruct((2 * room, rows, cols), send.dtype),
        scratch_shapes=[
            pltpu.VMEM((2, rows, cols), send.dtype),
            pltpu.VMEM((2, rows, cols), send.dtype),
            pltpu.VMEM((2, deep, rows, cols), send.dtype),
            pltpu.SemaphoreType.DMA((2,)),
            pltpu.SemaphoreType.DMA((2,)),
            pltpu.SemaphoreType.DMA((2, deep)),
            pltpu.SemaphoreType.DMA((2, count)),
        ],
        compiler_params=pltpu.CompilerParams(
            collective_id=step_id, has_side_effects=True, vmem_limit_bytes=40 * 1024 * 1024
        ),
    )(send, mask)


def lane_sum(x):
    def kernel(x_ref, out_ref, got, send_sem, recv_sem):
        across, beside = 1 - lax.axis_index("tensor"), 1 - lax.axis_index("sub")
        peers = ({"sub": beside}, {"tensor": across}, {"tensor": across, "sub": beside})
        barrier = pltpu.get_barrier_semaphore()
        for peer in peers:
            pl.semaphore_signal(barrier, inc=1, device_id=peer, device_id_type=pl.DeviceIdType.MESH)
        pl.semaphore_wait(barrier, 3)
        copies = [
            pltpu.make_async_remote_copy(
                src_ref=x_ref,
                dst_ref=got.at[k],
                send_sem=send_sem.at[k],
                recv_sem=recv_sem.at[k],
                device_id=peer,
                device_id_type=pl.DeviceIdType.MESH,
            )
            for k, peer in enumerate(peers)
        ]
        for copy in copies:
            copy.start()
        for copy in copies:
            copy.wait()
        near = x_ref[...].astype(jnp.float32) + got[0].astype(jnp.float32)
        out_ref[...] = near + (got[1].astype(jnp.float32) + got[2].astype(jnp.float32))

    vmem = pl.BlockSpec(memory_space=pltpu.VMEM)
    return pl.pallas_call(
        kernel,
        in_specs=[vmem],
        out_specs=vmem,
        out_shape=jax.ShapeDtypeStruct(x.shape, jnp.float32),
        scratch_shapes=[
            pltpu.VMEM((3, *x.shape), x.dtype),
            pltpu.SemaphoreType.DMA((3,)),
            pltpu.SemaphoreType.DMA((3,)),
        ],
        compiler_params=pltpu.CompilerParams(
            collective_id=20, has_side_effects=True, vmem_limit_bytes=40 * 1024 * 1024
        ),
    )(x)


def from_owners(x, owners):
    if owners > 4:
        return [y for y in lax.all_gather(x, "adapter", axis=0)], jnp.arange(owners)
    parts = [x]
    for shift in range(1, owners):
        ring = [(i, (i + shift) % owners) for i in range(owners)]
        parts.append(lax.ppermute(x, "adapter", ring))
    return parts, lax.rem(lax.axis_index("adapter") - jnp.arange(owners) + owners, owners)


def i32(x):
    return x.astype(jnp.int32)


def shards(tokens, frozen_weight, down_tables, up_tables, cotangent, block_owner, block_region):
    lane_index = lax.axis_index(("tensor", "sub"))
    owners = lax.axis_size("adapter")
    me = lax.axis_index("adapter")
    group = lax.axis_index("groups")
    tok_rows, d_part = tokens.shape
    reg_dev, _, rank_width = down_tables.shape
    key_portion = up_tables.shape[2]
    blocks = tok_rows // BLOCK
    slot_limit = max(2, blocks // owners * 2)
    tables = jnp.swapaxes(down_tables, 1, 2)

    region = block_owner[:, 0] * reg_dev + block_region
    named = lax.all_gather(region, ("groups", "adapter"), axis=0, tiled=True)
    named = named.reshape(-1, owners, blocks)
    named, up_tables = lax.optimization_barrier((named, up_tables))
    regions = owners * reg_dev
    present = i32(jnp.any(named[..., None] == jnp.arange(regions), axis=2))
    present = present.reshape(-1, owners, owners, reg_dev)
    counts = jnp.sum(present, axis=-1)
    apart = 1 - jnp.eye(owners, dtype=jnp.int32)
    need = jnp.max((counts + jnp.swapaxes(counts, 1, 2)) * apart)
    here = lax.dynamic_index_in_dim(present, group, 0, False)
    count = lax.dynamic_index_in_dim(counts, group, 0, False)
    before = jnp.arange(reg_dev)[:, None] < jnp.arange(reg_dev)[None, :]
    ranks = jnp.sum(here[..., :, None] * before, axis=-2)
    mine_in = lax.dynamic_index_in_dim(here, me, 0, False)
    mine_of = lax.dynamic_index_in_dim(here, me, 1, False)
    rank_in = lax.dynamic_index_in_dim(ranks, me, 0, False)
    rank_of = lax.dynamic_index_in_dim(ranks, me, 1, False)
    count_in = lax.dynamic_index_in_dim(count, me, 0, False)
    count_of = lax.dynamic_index_in_dim(count, me, 1, False)

    j = jnp.arange(blocks)
    less = region[:, None] < region[None, :]
    tie = (region[:, None] == region[None, :]) & (j[:, None] < j[None, :])
    place = jnp.sum(i32(less | tie), axis=0)
    order = jnp.sum(i32(place[:, None] == j[None, :]) * j[:, None], axis=0)
    first = jnp.sum(i32(less), axis=0)
    slot = jnp.sum(i32(place[:, None] == j[None, :]) * first[:, None], axis=0)
    term_slot = jnp.sum(i32(region[:, None] < jnp.arange(regions)[None, :]), axis=0)
    term_slot = jnp.minimum(term_slot, blocks - 1).reshape(owners, reg_dev)

    up_parts, up_place = from_owners(up_tables, owners)
    up_all = jnp.concatenate(up_parts, axis=0)
    up_at = jnp.sum(i32(block_owner == jnp.arange(owners)) * up_place, axis=1) * reg_dev + block_region
    up_part = up_down_parts(up_at, up_all, cotangent)
    if lax.axis_size("tensor") == 2 and lax.axis_size("sub") == 2:
        low_up = lane_sum(up_part)
    else:
        low_up = lax.psum(up_part, ("tensor", "sub")).astype(jnp.float32)
    low_up = (adapter_scale * low_up).astype(jnp.bfloat16)
    terms = summed_terms(order, slot, low_up, tokens, 1.0)

    frozen_weight, up_all = lax.optimization_barrier((frozen_weight, up_all))
    weights, weight_place = from_owners(frozen_weight, owners)
    weight = jnp.concatenate(weights, axis=1)
    lanes = lax.axis_size("tensor") * lax.axis_size("sub")
    up_blocks = jnp.take(up_all, up_at, axis=0, mode="clip")
    up_wide = lax.all_to_all(
        up_blocks, ("tensor", "sub"), split_axis=0, concat_axis=2, tiled=True
    )

    def line_tracks(w):
        base = jnp.stack([
            jnp.stack([w[0, 0] * 0, w[0, 3] + w[0, 2], w[0, 3], w[0, 0] * 0]),
            jnp.stack([w[0, 3] + w[0, 2], w[0, 0] * 0, w[0, 3] + w[0, 2] + w[1, 3], w[0, 3] + w[0, 2]]),
            jnp.stack([w[0, 3], w[0, 3] + w[0, 2] + w[1, 3], w[0, 0] * 0, w[0, 3]]),
            jnp.stack([w[0, 0] * 0, w[0, 3] + w[0, 2], w[0, 3], w[0, 0] * 0]),
        ])
        row = lax.dynamic_index_in_dim(base, me, 0, False)
        jumps = (me + jnp.arange(owners) == 5)[:, None]

        def track(k):
            return row[:, None] + k + jnp.where(jumps & (k >= w[0, 2]), w[1, 3], 0)

        return track

    peer = jnp.arange(owners)
    if owners == 4:
        full = blocks * owners
        sizes = sorted({-(-full * f // 64) for f in (26, 27, 28, 29, 30, 32, 36, 64)})
        both = counts + jnp.swapaxes(counts, 1, 2)
        loads = []
        for cut in range(owners - 1):
            over = i32((peer[:, None] <= cut) & (peer[None, :] > cut))
            loads.append(jnp.max(jnp.sum(both * over, axis=(1, 2))))
        need = jnp.max(jnp.stack(loads))
        track = line_tracks(count + count.T)
        ways = jnp.stack([peer > me, peer < me])
        side = jnp.where(peer < me, 0, full)[:, None]
    else:
        full = 2 * slot_limit
        sizes = sorted({-(-full * f // 16) for f in (8, 10, 12, 16)})
        ways = jnp.eye(owners, dtype=jnp.int32) * i32(peer != me)
        side = (peer * full)[:, None]

        def track(k):
            return k

    t = jnp.arange(full)
    takes_table = mine_of[:, :, None] * i32(track(rank_of)[:, :, None] == t)
    takes_term = mine_in[:, :, None] * i32(track(count_of[:, None] + rank_in)[:, :, None] == t)
    takes_table = i32(ways)[:, :, None, None] * takes_table
    takes_term = i32(ways)[:, :, None, None] * takes_term
    table_at = jnp.sum(takes_table * jnp.arange(reg_dev)[:, None], axis=(1, 2))
    term_at = jnp.sum(takes_term * term_slot[:, :, None], axis=(1, 2))
    has_table = jnp.sum(takes_table, axis=(1, 2))
    has_term = jnp.sum(takes_term, axis=(1, 2))
    kind = i32(jnp.where(has_table > 0, 0, jnp.where(has_term > 0, 1, 2)))
    branch = jnp.sum(i32(need > jnp.array(sizes[:-1], jnp.int32)))

    def exchange(index, tracks, table_at, term_at, kind, tables, terms):
        table_at, term_at, kind = [x[:, :tracks].reshape(-1) for x in (table_at, term_at, kind)]
        send = pack(table_at, term_at, kind, tables, terms)
        if owners == 4:
            parts = 2
            mask = jnp.repeat(i32(kind < 2), parts)
            send = send.reshape(2 * tracks * parts, rank_width // parts, d_part)
            got = line_exchange(tracks * parts, index, full * parts, send, mask)
            return got.reshape(2 * full, rank_width, d_part)
        got = lax.all_to_all(
            send.reshape(owners, tracks, rank_width, d_part),
            "adapter", split_axis=0, concat_axis=0, tiled=True,
        )
        got = jnp.pad(got, ((0, 0), (0, full - tracks), (0, 0), (0, 0)))
        return got.reshape(owners * full, rank_width, d_part)

    bodies = [functools.partial(exchange, i, n) for i, n in enumerate(sizes)]
    got = lax.switch(branch, bodies, table_at, term_at, kind, tables, terms)

    flat = (side + track(rank_in)).reshape(-1)
    own = i32(block_owner[:, 0] == me)
    got_at = jnp.sum(i32(region[:, None] == jnp.arange(regions)) * flat, axis=1) * (1 - own)
    remote = mine_of.T * (1 - i32(peer == me))
    back_at = (side + track(count_in[:, None] + rank_of)).T
    own_terms = lax.dynamic_index_in_dim(mine_in, me, 0, False)
    own_slots = lax.dynamic_index_in_dim(term_slot, me, 0, False)
    valid = jnp.concatenate([remote, own_terms[:, None]], axis=1)
    inner = inner_parts(got_at, block_region * own, own, got, tables, tokens)
    low_down = lax.psum(inner, ("tensor", "sub"))
    grad_down = owner_sum(back_at * remote, own_slots * own_terms, valid, got, terms, reg_dev)
    frozen_part = jnp.dot(tokens, weight, preferred_element_type=jnp.float32).astype(jnp.bfloat16)

    frozen_sum = lax.psum_scatter(
        frozen_part, ("tensor", "sub"), scatter_dimension=0, tiled=True
    )
    mine = tok_rows // lanes
    low_mine = lax.dynamic_slice_in_dim(low_down, lane_index * mine, mine, 1)
    low_mine = low_mine.reshape(rank_width, mine // BLOCK, BLOCK)
    lora = adapter_scale * jnp.einsum(
        "rbt,brk->btk", low_mine, up_wide, preferred_element_type=jnp.float32
    )
    width = frozen_weight.shape[1]
    frozen_sum = jnp.concatenate(
        [lax.dynamic_slice_in_dim(frozen_sum, weight_place[o] * width, width, 1) for o in range(owners)],
        axis=1,
    )
    projected = (frozen_sum.astype(jnp.float32) + lora.reshape(frozen_sum.shape)).astype(jnp.bfloat16)

    up_terms = summed_terms(order, slot, low_down, cotangent, adapter_scale)
    s = jnp.arange(slot_limit)
    takes = mine_in[:, :, None] * i32(rank_in[:, :, None] == s)
    term_at = jnp.sum(takes * term_slot[:, :, None], axis=1).reshape(-1)
    up_send = jnp.take(up_terms, term_at, axis=0, mode="clip")
    up_got = lax.all_to_all(
        up_send.reshape(owners, slot_limit, rank_width, key_portion),
        "adapter", split_axis=0, concat_axis=0, tiled=True,
    ).reshape(owners * slot_limit, rank_width, key_portion)
    back_at = (jnp.arange(owners) * slot_limit)[None, :] + jnp.minimum(rank_of.T, slot_limit - 1)
    valid = jnp.concatenate([mine_of.T, jnp.zeros((reg_dev, 1), jnp.int32)], axis=1)
    grad_up = owner_sum(
        back_at * mine_of.T, jnp.zeros((reg_dev,), jnp.int32), valid, up_got, up_got, reg_dev
    )
    return (projected, jnp.swapaxes(grad_down, 1, 2), grad_up)


def solution(mesh):
    return jax.shard_map(
        shards,
        mesh=mesh,
        in_specs=(
            P(("groups", "adapter"), ("tensor", "sub")),
            P(("tensor", "sub"), "adapter"),
            P("adapter", ("tensor", "sub"), None),
            P("adapter", None, ("tensor", "sub")),
            P(("groups", "adapter"), ("tensor", "sub")),
            P(("groups", "adapter"), None),
            P(("groups", "adapter")),
        ),
        out_specs=(
            P(("groups", "adapter", "tensor", "sub"), None),
            P(("groups", "adapter"), ("tensor", "sub"), None),
            P(("groups", "adapter"), None, ("tensor", "sub")),
        ),
        check_vma=False,
    )
```
